32 devices in a mesh: gx: 16 (over z, y, core), gy: 2 (over x).
Axes of the slice: x: 2, y: 2, z: 4, core: 2. Of those that a mesh axis runs over, the one named last changes fastest.
Arguments:
- pops: float32 [19, 64, 16, 128], P(None, 'gx', 'gy'), may hold values from 0.005 to 0.5, as said below
- label: int32 [64, 16, 128], P('gx', 'gy'), may hold values from 0 to 2, as said below
- drive: float32 [3, 64, 16, 128], P(None, 'gx', 'gy'), may hold values from -0.3 to 0.3
Outputs:
- momentum: float32 [3, 64, 16, 128], P(None, 'gx', 'gy')
- running: float32 [3, 16, 4, 32], P(None, 'gx', 'gy')
The draws below stay inside these ranges and needn't reach their ends.
Inputs may be any that keep to these rules, and one draw needn't show every extreme that they name: `pops`: populations near a local equilibrium with density 0.8 to 1.2 and each velocity component within 0.1. `label`: 2 marks walls: every cell with z index 0 or 127, and scattered obstacle cells; elsewhere 1 marks the second solution, 0 the first.
All inputs are finite; a program needn't handle non-finite values.
Results may differ from the reference program's by a relative error of at most 0.0003.
Values sent between devices are 32-bit elements; how exact they have to be, the bound alone decides.
A program may use at most 64 MiB of HBM per device.

```python
import math
import jax
import jax.numpy as jnp

NZ = 128
STEPS = 4
NX = 64
NY = 16
SX = 16
SY = 4
SZ = 32


VELOCITY = [[0, 0, 0], [1, 0, 0], [-1, 0, 0], [0, 1, 0], [0, -1, 0], [0, 0, 1], [0, 0, -1], [1, 1, 0], [-1, -1, 0], [1, -1, 0], [-1, 1, 0], [1, 0, 1], [-1, 0, -1], [1, 0, -1], [-1, 0, 1], [0, 1, 1], [0, -1, -1], [0, 1, -1], [0, -1, 1]]


WEIGHTS = [1.0 / 3.0] + [1.0 / 18.0] * 6 + [1.0 / 36.0] * 12


def draw_pops(key, part):
    density = 1.0 + 0.2 * jax.random.uniform(jax.random.fold_in(key, 11), (NX, NY, NZ), jnp.float32, -1.0, 1.0)
    rough = 0.1 * jax.random.uniform(jax.random.fold_in(key, 12), (3, NX, NY, NZ), jnp.float32, -1.0, 1.0)
    speed = rough
    columns = [jnp.array([row[axis_id] for row in VELOCITY], jnp.float32).reshape(19, 1, 1, 1) for axis_id in range(3)]
    weights = jnp.array(WEIGHTS, jnp.float32).reshape(19, 1, 1, 1)
    along = columns[0] * speed[0] + columns[1] * speed[1] + columns[2] * speed[2]
    square = speed[0] * speed[0] + speed[1] * speed[1] + speed[2] * speed[2]
    balance = weights * density * (1.0 + 3.0 * along + 4.5 * along * along - 1.5 * square)
    noise = 1.0 + 0.1 * jax.random.uniform(jax.random.fold_in(key, 13), (19, NX, NY, NZ), jnp.float32, -1.0, 1.0)
    return (balance * noise).astype(jnp.float32)


def draw_label(key, part):
    offsets = jax.random.randint(jax.random.fold_in(key, 21), (NX, 1, 1), -(NY // 4), NY // 4 + 1)
    rows = jnp.arange(NY, dtype=jnp.int32).reshape(1, NY, 1)
    depth = jnp.arange(NZ, dtype=jnp.int32).reshape(1, 1, NZ)
    second = (rows >= NY // 2 + offsets).astype(jnp.int32) + jnp.zeros((NX, NY, NZ), jnp.int32)
    obstacle = jax.random.randint(jax.random.fold_in(key, 22), (NX, NY, NZ), 0, 64) == 0
    wall = jnp.logical_or(jnp.logical_or(depth == 0, depth == NZ - 1), obstacle)
    return jnp.where(wall, 2, second).astype(jnp.int32)


def levels(stream_key, dims, cuts, least, high):
    def one(axis_at, shards_of):
        heights = jax.random.uniform(jax.random.fold_in(jax.random.fold_in(stream_key, 6), axis_at), (shards_of,), jnp.float32, least / len(cuts), high / len(cuts))
        return jnp.repeat(jnp.exp(heights), dims[axis_at] // shards_of).reshape((-1,) + (1,) * (len(dims) - axis_at - 1))

    gain = one(*cuts[0])
    for cut in cuts[1:]:
        gain = gain * one(*cut)
    return gain


def bell_draw(rng, dims, width, limit, cuts=(), kind=jnp.bfloat16):
    values = width * jax.random.normal(rng, dims, jnp.float32)
    if cuts:
        values = values * levels(rng, dims, cuts, -0.22, 0.18)
    return jnp.clip(values, -limit, limit).astype(kind)


def setup_inputs(seed: int = 0) -> dict:
    arg_keys = jax.random.split(jax.random.key(seed), 4)
    pops = draw_pops(jax.random.fold_in(arg_keys[3], 71), 0)
    label = draw_label(jax.random.fold_in(arg_keys[3], 71), 0)
    drive = bell_draw(arg_keys[2], (3, NX, NY, NZ), 0.05, 0.3, ((1, 16), (2, 2)), jnp.float32)
    return {"pops": pops, "label": label, "drive": drive}


VELOCITY = [[0, 0, 0], [1, 0, 0], [-1, 0, 0], [0, 1, 0], [0, -1, 0], [0, 0, 1], [0, 0, -1],
            [1, 1, 0], [-1, -1, 0], [1, -1, 0], [-1, 1, 0], [1, 0, 1], [-1, 0, -1], [1, 0, -1], [-1, 0, 1],
            [0, 1, 1], [0, -1, -1], [0, 1, -1], [0, -1, 1]]
OPPOSITE = [0, 2, 1, 4, 3, 6, 5, 8, 7, 10, 9, 12, 11, 14, 13, 16, 15, 18, 17]
WEIGHTS = [1.0 / 3.0] + [1.0 / 18.0] * 6 + [1.0 / 36.0] * 12
PAIRS = [(0, 0), (1, 1), (2, 2), (0, 1), (0, 2), (1, 2)]
COMPONENT = [[0, 3, 4], [3, 1, 5], [4, 5, 2]]
SLOW_VISCOSITY = 0.0004


def collide(pops, label, drive, phase):
    columns = [jnp.array([row[axis_id] for row in VELOCITY], jnp.float32).reshape(19, 1, 1, 1) for axis_id in range(3)]
    weights = jnp.array(WEIGHTS, jnp.float32).reshape(19, 1, 1, 1)
    density = jnp.sum(pops, axis=0)
    moment = [jnp.sum(columns[axis_id] * pops, axis=0) for axis_id in range(3)]
    speed = [moment[axis_id] / density for axis_id in range(3)]
    along = columns[0] * speed[0] + columns[1] * speed[1] + columns[2] * speed[2]
    square = speed[0] * speed[0] + speed[1] * speed[1] + speed[2] * speed[2]
    balance = weights * density * (1.0 + 3.0 * along + 4.5 * along * along - 1.5 * square)
    second = label == 1
    solid = label == 2
    omega = jnp.where(second, 1.1, 1.6)
    strength = jnp.where(second, 0.6, 1.0) * phase
    push = columns[0] * drive[0] + columns[1] * drive[1] + columns[2] * drive[2]
    relaxed = pops - omega * (pops - balance) + 3.0 * weights * strength * push
    bounced = jnp.stack([pops[other] for other in OPPOSITE])
    post = jnp.where(solid, bounced, relaxed)
    fluid = jnp.where(solid, 0.0, 1.0)
    stress = jnp.stack([moment[first] * moment[later] / density * fluid for first, later in PAIRS])
    return post, stress


def momentum_of(pops):
    columns = [jnp.array([row[axis_id] for row in VELOCITY], jnp.float32).reshape(19, 1, 1, 1) for axis_id in range(3)]
    return jnp.stack([jnp.sum(columns[axis_id] * pops, axis=0) for axis_id in range(3)])


def reference(pops, label, drive):
    state = pops
    total = jnp.zeros((6,) + pops.shape[1:], jnp.float32)
    for step in range(STEPS):
        phase = math.cos(2.0 * math.pi * (step + 0.5) / STEPS)
        post, stress = collide(state, label, drive, phase)
        total = total + stress
        state = jnp.stack([jnp.roll(post[index], (VELOCITY[index][0], VELOCITY[index][1], VELOCITY[index][2]), axis=(0, 1, 2)) for index in range(19)])
    momentum = momentum_of(state)
    slow = (total / STEPS).reshape(6, SX, 4, SY, 4, SZ, 4).mean(axis=(2, 4, 6))
    spectrum = jnp.fft.fftn(slow, axes=(1, 2, 3))
    wave_x = (2.0 * math.pi * jnp.fft.fftfreq(SX)).reshape(SX, 1, 1)
    wave_y = (2.0 * math.pi * jnp.fft.fftfreq(SY)).reshape(1, SY, 1)
    wave_z = (2.0 * math.pi * jnp.fft.fftfreq(SZ)).reshape(1, 1, SZ)
    waves = [wave_x, wave_y, wave_z]
    force = [-1j * (waves[0] * spectrum[COMPONENT[first][0]] + waves[1] * spectrum[COMPONENT[first][1]] + waves[2] * spectrum[COMPONENT[first][2]]) for first in range(3)]
    wave_sq = wave_x * wave_x + wave_y * wave_y + wave_z * wave_z
    positive = wave_sq > 0
    safe = jnp.where(positive, wave_sq, 1.0)
    inner = waves[0] * force[0] + waves[1] * force[1] + waves[2] * force[2]
    velocity = jnp.stack([jnp.where(positive, (force[first] - waves[first] * inner / safe) / (SLOW_VISCOSITY * safe), 0.0) for first in range(3)])
    running = jnp.real(jnp.fft.ifftn(velocity, axes=(1, 2, 3))).astype(jnp.float32)
    return momentum, running
```

```python
import functools
import math

import jax
import jax.numpy as jnp
import numpy as np
from jax import lax
from jax.experimental import pallas as pl
from jax.experimental.pallas import tpu as pltpu
from jax.sharding import PartitionSpec as P

MESH = pl.DeviceIdType.MESH
NZ = 128
STEPS = 4
CUT = 4
VELOCITY = [
    (0, 0, 0),
    (1, 0, 0),
    (-1, 0, 0),
    (0, 1, 0),
    (0, -1, 0),
    (0, 0, 1),
    (0, 0, -1),
    (1, 1, 0),
    (-1, -1, 0),
    (1, -1, 0),
    (-1, 1, 0),
    (1, 0, 1),
    (-1, 0, -1),
    (1, 0, -1),
    (-1, 0, 1),
    (0, 1, 1),
    (0, -1, -1),
    (0, 1, -1),
    (0, -1, 1),
]
WEIGHTS = [1.0 / 3.0] + [1.0 / 18.0] * 6 + [1.0 / 36.0] * 12
SLOW_VISCOSITY = 0.0004
PAIRS = [(0, 0), (1, 1), (2, 2), (0, 1), (0, 2), (1, 2)]
EVEN = 4
CROSS = {
    (axis, sign): [i for i in range(19) if VELOCITY[i][axis] == sign] for axis in (0, 1) for sign in (1, -1)
}
MESSAGES = 8


def wave_table(length):
    index = np.arange(length)
    return 2.0 * np.pi * np.where(index >= (length + 1) // 2, index - length, index) / length


def response(nx, ny, nz):
    waves = np.meshgrid(wave_table(nx), wave_table(ny), wave_table(nz), indexing="ij")
    square = waves[0] ** 2 + waves[1] ** 2 + waves[2] ** 2
    safe = np.where(square > 0, square, 1.0)
    out = np.zeros((3, 6, nx, ny, nz // 2 + 1), np.complex128)
    for c, (p, q) in enumerate(PAIRS):
        force = [np.zeros_like(square) for _ in range(3)]
        force[p] = force[p] + waves[q]
        if p != q:
            force[q] = force[q] + waves[p]
        inner = sum(waves[a] * force[a] for a in range(3))
        for a in range(3):
            gain = np.where(square > 0, (force[a] - waves[a] * inner / safe) / (SLOW_VISCOSITY * safe), 0.0)
            mirror = np.roll(gain[::-1, ::-1, ::-1], (1, 1, 1), (0, 1, 2))
            odd = 0.5 * (gain - mirror)
            out[a, c] = np.fft.ifft2(-1j * odd, axes=(0, 1))[:, :, : nz // 2 + 1]
    return out


def tables(nx, ny):
    slow = NZ // CUT
    half = slow // 2
    green = response(nx, 2 * ny, slow)
    count = nx * ny
    send = np.zeros((count, 12, 2, 4, slow))
    place = {(0, 0): (0, 0), (0, 1): (0, 1), (2, 0): (0, 2), (2, 1): (0, 3), (1, 0): (1, 0), (1, 1): (1, 1)}
    far_x = np.arange(count) // ny
    far_y = np.arange(count) % ny
    for c in range(6):
        for half_y in range(2):
            for (a, to_y), (row, block) in place.items():
                g = green[a, c][far_x, (2 * far_y + to_y - half_y) % (2 * ny)]
                inside = g[:, 1:half]
                if a < 2:
                    inside = inside.real if c < EVEN else inside.imag
                else:
                    inside = inside.imag if c < EVEN else -inside.real
                send[:, 2 * c + half_y, row, block, : half + 1] = g.real
                send[:, 2 * c + half_y, row, block, 1:half] = inside
                send[:, 2 * c + half_y, row, block, half + 1 :] = inside
    send = send.reshape(count // 4, 4, 12, 2, NZ).transpose(0, 2, 1, 3, 4).reshape(count // 4, 12, 8, NZ)
    place_z = np.arange(slow)
    angle = 2.0 * np.pi * place_z[:, None] * np.arange(half + 1)[None, :] / slow
    cosine, sine = np.cos(angle), np.sin(angle)
    plain = np.concatenate([cosine, -sine[:, 1:half]], axis=1)
    turned = np.concatenate([cosine[:, :1], sine[:, 1:half], cosine[:, half:], cosine[:, 1:half]], axis=1)
    scale = 1.0 / (STEPS * CUT**3)
    forward = np.concatenate([np.tile(plain, (CUT, 1, 4)).reshape(CUT, slow, NZ).transpose(1, 0, 2).reshape(NZ, NZ),
                              np.tile(turned, (CUT, 1, 4)).reshape(CUT, slow, NZ).transpose(1, 0, 2).reshape(NZ, NZ)], axis=1)
    forward = forward * scale
    edge = [cosine[:, :1], cosine[:, half:]]
    back = np.concatenate([edge[0], 2 * cosine[:, 1:half], edge[1], -2 * sine[:, 1:half]], axis=1).T / slow
    back_turned = np.concatenate([edge[0], -2 * sine[:, 1:half], edge[1], -2 * cosine[:, 1:half]], axis=1).T / slow
    inverse = np.concatenate([back, back, back_turned, back_turned], axis=0)
    inverse = np.concatenate([inverse, np.zeros((NZ, NZ - slow))], axis=1)
    return send.astype(np.float32), forward.astype(np.float32), inverse.astype(np.float32)


def dot(left, right):
    return jnp.dot(left, right, precision=lax.Precision.HIGHEST, preferred_element_type=jnp.float32)


def moments(f):
    rho = f[0]
    for i in range(1, 19):
        rho = rho + f[i]
    j = []
    for axis in range(3):
        plus = [f[i] for i in range(19) if VELOCITY[i][axis] == 1]
        minus = [f[i] for i in range(19) if VELOCITY[i][axis] == -1]
        total = plus[0] - minus[0]
        for one, other in zip(plus[1:], minus[1:]):
            total = total + (one - other)
        j.append(total)
    return rho, j


def collide(f, rho, j, inverse, keep, omega, push, solid):
    speed = [one * inverse for one in j]
    square = speed[0] * speed[0] + speed[1] * speed[1] + speed[2] * speed[2]
    weight = omega * rho
    base = weight * (1.0 - 1.5 * square)
    quad = 4.5 * weight
    lead = [3.0 * (omega * j[a] + push[a]) for a in range(3)]
    post = [None] * 19
    post[0] = jnp.where(solid, f[0], keep * f[0] + WEIGHTS[0] * base)
    for i in range(1, 19, 2):
        along = linear = None
        for axis in range(3):
            c = VELOCITY[i][axis]
            if c:
                along = c * speed[axis] if along is None else along + speed[axis] if c > 0 else along - speed[axis]
                linear = c * lead[axis] if linear is None else linear + lead[axis] if c > 0 else linear - lead[axis]
        even = WEIGHTS[i] * (base + quad * (along * along))
        odd = WEIGHTS[i] * linear
        post[i] = jnp.where(solid, f[i + 1], keep * f[i] + (even + odd))
        post[i + 1] = jnp.where(solid, f[i], keep * f[i + 1] + (even - odd))
    return post


def kernel(
    nx, ny, pops_hbm, label_hbm, drive_hbm, table_hbm, forward_hbm, inverse_hbm, momentum_hbm, running_ref,
    state, label, drive, table, forward, inverse_z, momentum, face_out, face_in, row_out, row_in, edge_out, edge_in,
    message, arrived, load_sem, const_sem, halo_send, halo_recv, slow_send, slow_recv, out_sem,
):
    width = label.shape[0]
    gx = lax.axis_index("gx")
    gy = lax.axis_index("gy")
    count = nx * ny

    loads = [
        pltpu.make_async_copy(pops_hbm, state.at[0], load_sem.at[0]),
        pltpu.make_async_copy(label_hbm, label, load_sem.at[1]),
        pltpu.make_async_copy(drive_hbm, drive, load_sem.at[2]),
    ]
    constants = [
        pltpu.make_async_copy(table_hbm, table, const_sem.at[0]),
        pltpu.make_async_copy(forward_hbm, forward, const_sem.at[1]),
        pltpu.make_async_copy(inverse_hbm, inverse_z, const_sem.at[2]),
    ]
    for copy in loads + constants:
        copy.start()

    def device_at(far):
        return (lax.rem(gx + far // ny, nx), lax.rem(gy + far % ny, ny))

    def over_others(body):
        if count <= 64:
            for far in range(1, count):
                body(far)
        else:
            def step(far, carry):
                body(far)
                return carry

            lax.fori_loop(1, count, step, 0)

    barrier = pltpu.get_barrier_semaphore()
    over_others(lambda far: pl.semaphore_signal(barrier, inc=1, device_id=device_at(far), device_id_type=MESH))

    for copy in loads:
        copy.wait()

    east, west = lax.rem(gx + 1, nx), lax.rem(gx + nx - 1, nx)
    north, south = lax.rem(gy + 1, ny), lax.rem(gy + ny - 1, ny)
    side_x = {1: east, -1: west}
    side_y = {1: north, -1: south}
    slot = {1: 0, -1: 1}

    def remote(src, dst, step, number, place):
        return pltpu.make_async_remote_copy(
            src_ref=src,
            dst_ref=dst,
            send_sem=halo_send.at[step, number],
            recv_sem=halo_recv.at[step, number],
            device_id=place,
            device_id_type=MESH,
        )

    def halo(step):
        copies = []
        for sign in (1, -1):
            s = slot[sign]
            copies.append(remote(face_out.at[step, s], face_in.at[step, s], step, s, (side_x[sign], gy)))
        if ny == 2:
            copies.append(remote(row_out.at[step], row_in.at[step], step, 2, (gx, north)))
            for sign in (1, -1):
                s = slot[sign]
                copies.append(remote(edge_out.at[step, s], edge_in.at[step, s], step, 4 + s, (side_x[sign], north)))
        else:
            for sign in (1, -1):
                s = slot[sign]
                copies.append(remote(row_out.at[step, s], row_in.at[step, s], step, 2 + s, (gx, side_y[sign])))
                for turn in (1, -1):
                    t = slot[turn]
                    copies.append(
                        remote(
                            edge_out.at[step, t, s], edge_in.at[step, t, s], step, 4 + 2 * t + s,
                            (side_x[turn], side_y[sign]),
                        )
                    )
        return copies

    row_id = lax.broadcasted_iota(jnp.int32, (8, NZ), 0)
    first_row = row_id == 0
    last_row = row_id == 7

    def read(step, i, p):
        cx, cy, _ = VELOCITY[i]
        if step == 0:
            return state[0, i, p]
        outside = (cx == 1 and p == 0) or (cx == -1 and p == width - 1)
        if outside:
            value = face_in[step - 1, slot[cx], CROSS[0, cx].index(i)]
        else:
            value = state[step % 2, i, p]
        if cy:
            if outside:
                row = edge_in[step - 1, slot[cx], slot[cy]]
            else:
                row = row_in[step - 1, slot[cy], CROSS[1, cy].index(i) * width + p]
            value = jnp.where(first_row if cy == 1 else last_row, jnp.broadcast_to(row, (8, NZ)), value)
        return value

    def write(step, i, p, value):
        cx, cy, cz = VELOCITY[i]
        if cz:
            value = pltpu.roll(value, cz % NZ, 1)
        if cy:
            value = pltpu.roll(value, cy % 8, 0)
            line = value[0:1] if cy == 1 else value[7:8]
        outside = (cx == 1 and p == width - 1) or (cx == -1 and p == 0)
        if outside:
            face_out[step, slot[cx], CROSS[0, cx].index(i)] = value
            if cy:
                edge_out[step, slot[cx], slot[cy]] = line
        else:
            state[(step + 1) % 2, i, p + cx] = value
            if cy:
                row_out[step, slot[cy], CROSS[1, cy].index(i) * width + p + cx] = line

    def send_copy(far):
        return pltpu.make_async_remote_copy(
            src_ref=message.at[far],
            dst_ref=arrived.at[far],
            send_sem=slow_send,
            recv_sem=slow_recv,
            device_id=device_at(far),
            device_id_type=MESH,
        )

    total = [None] * 6
    copies = []
    for step in range(STEPS):
        phase = math.cos(2.0 * math.pi * (step + 0.5) / STEPS)
        if step:
            for copy in copies:
                copy.wait_recv()
        held = []
        for p in range(width):
            f = [read(step, i, p) for i in range(19)]
            rho, j = moments(f)
            inverse = 1.0 / rho
            kind = label[p]
            solid = kind == 2
            thin = jnp.where(solid, 0.0, inverse)
            scaled = [one * thin for one in j]
            for c, (a, b) in enumerate(PAIRS):
                term = scaled[a] * j[b]
                total[c] = term if total[c] is None else total[c] + term
            if step == STEPS - 1:
                held.append((rho, j, inverse))
                continue
            second = kind == 1
            omega = jnp.where(second, 1.1, 1.6)
            strength = jnp.where(second, 0.6 * phase, phase)
            push = [strength * drive[a, p] for a in range(3)]
            post = collide(f, rho, j, inverse, 1.0 - omega, omega, push, solid)
            for i in range(19):
                write(step, i, p, post[i])
        if step == STEPS - 1:
            for copy in constants:
                copy.wait()
            plain = dot(jnp.concatenate(total[:EVEN], axis=0), forward[:, :NZ])
            turned = dot(jnp.concatenate(total[EVEN:], axis=0), forward[:, NZ:])
            lines = []
            for c in range(6):
                source = plain if c < EVEN else turned
                tile = source[8 * c : 8 * c + 8] if c < EVEN else source[8 * (c - EVEN) : 8 * (c - EVEN) + 8]
                tile = tile + pltpu.roll(tile, 7, 0)
                tile = tile + pltpu.roll(tile, 6, 0)
                lines.append(jnp.broadcast_to(tile[0:1], (8, NZ)))
                lines.append(jnp.broadcast_to(tile[4:5], (8, NZ)))

            def group(g):
                value = lines[0] * table[g, 0]
                for k in range(1, 12):
                    value = value + lines[k] * table[g, k]
                for k in range(4):
                    message[4 * g + k] = value[2 * k : 2 * k + 2]

            if count <= 64:
                for g in range(count // 4):
                    group(g)
            else:
                def each(g, carry):
                    group(g)
                    return carry

                lax.fori_loop(0, count // 4, each, 0)
            over_others(lambda far: send_copy(far).start())
            for p in range(width):
                f = [read(step, i, p) for i in range(19)]
                rho, j, inverse = held[p]
                kind = label[p]
                second = kind == 1
                omega = jnp.where(second, 1.1, 1.6)
                strength = jnp.where(second, 0.6 * phase, phase)
                push = [strength * drive[a, p] for a in range(3)]
                post = collide(f, rho, j, inverse, 1.0 - omega, omega, push, kind == 2)
                for i in range(19):
                    write(step, i, p, post[i])
        elif step == 0:
            pl.semaphore_wait(barrier, count - 1)
        for copy in copies:
            copy.wait_send()
        copies = halo(step)
        for copy in copies:
            copy.start()

    for copy in copies:
        copy.wait_recv()
    for p in range(width):
        f = [None] + [read(STEPS, i, p) for i in range(1, 19)]
        for axis in range(3):
            value = None
            for i in range(1, 19):
                c = VELOCITY[i][axis]
                if c:
                    value = c * f[i] if value is None else value + f[i] if c > 0 else value - f[i]
            momentum[axis, p] = value
    out_copy = pltpu.make_async_copy(momentum, momentum_hbm, out_sem)
    out_copy.start()
    for copy in copies:
        copy.wait_send()

    rest = pl.ds(1, count - 1)
    pltpu.make_async_copy(message.at[rest], arrived.at[rest], slow_recv).wait()
    spectrum = message[0]
    if count <= 64:
        for far in range(1, count):
            spectrum = spectrum + arrived[far]
    else:
        spectrum = lax.fori_loop(1, count, lambda far, value: value + arrived[far], spectrum)
    upper = jnp.broadcast_to(spectrum[0:1], (8, NZ))
    lower = jnp.broadcast_to(spectrum[1:2], (8, NZ))
    lane = lax.broadcasted_iota(jnp.int32, (8, NZ), 1)
    slow_z = NZ // CUT
    block = row_id % 2 + jnp.where(row_id >= 4, 2, 0)
    low = slow_z * block
    spread = jnp.where((row_id == 2) | (row_id == 3), lower, upper)
    spread = jnp.where((lane >= low) & (lane < low + slow_z), spread, 0.0)
    result = dot(spread, inverse_z[...])
    for a in range(3):
        running_ref[a, 0] = result[2 * a : 2 * a + 2, :slow_z]
    pltpu.make_async_copy(arrived.at[rest], message.at[rest], slow_send).wait()
    out_copy.wait()


def local(nx, ny, constants, pops, label, drive):
    width, height = pops.shape[1], pops.shape[2]
    count = nx * ny
    send, forward, inverse = constants
    anywhere = pl.BlockSpec(memory_space=pl.ANY)
    f32 = jnp.float32
    return pl.pallas_call(
        functools.partial(kernel, nx, ny),
        out_shape=(
            jax.ShapeDtypeStruct((3, width, height, NZ), f32),
            jax.ShapeDtypeStruct((3, width // CUT, height // CUT, NZ // CUT), f32),
        ),
        in_specs=[anywhere] * 6,
        out_specs=(anywhere, pl.BlockSpec(memory_space=pltpu.VMEM)),
        scratch_shapes=[
            pltpu.VMEM((2, 19, width, height, NZ), f32),
            pltpu.VMEM((width, height, NZ), jnp.int32),
            pltpu.VMEM((3, width, height, NZ), f32),
            pltpu.VMEM(send.shape, f32),
            pltpu.VMEM(forward.shape, f32),
            pltpu.VMEM(inverse.shape, f32),
            pltpu.VMEM((3, width, height, NZ), f32),
            pltpu.VMEM((STEPS, 2, 5, height, NZ), f32),
            pltpu.VMEM((STEPS, 2, 5, height, NZ), f32),
            pltpu.VMEM((STEPS, 2, 5 * width, 1, NZ), f32),
            pltpu.VMEM((STEPS, 2, 5 * width, 1, NZ), f32),
            pltpu.VMEM((STEPS, 2, 2, 1, NZ), f32),
            pltpu.VMEM((STEPS, 2, 2, 1, NZ), f32),
            pltpu.VMEM((count, 2, NZ), f32),
            pltpu.VMEM((count, 2, NZ), f32),
            pltpu.SemaphoreType.DMA((3,)),
            pltpu.SemaphoreType.DMA((3,)),
            pltpu.SemaphoreType.DMA((STEPS, MESSAGES)),
            pltpu.SemaphoreType.DMA((STEPS, MESSAGES)),
            pltpu.SemaphoreType.DMA,
            pltpu.SemaphoreType.DMA,
            pltpu.SemaphoreType.DMA,
        ],
        compiler_params=pltpu.CompilerParams(
            collective_id=0, has_side_effects=True, vmem_limit_bytes=32 * 1024 * 1024
        ),
        name="cycle",
    )(pops, label, drive, send, forward, inverse)


def solution(mesh):
    nx, ny = mesh.shape["gx"], mesh.shape["gy"]
    constants = tuple(jnp.asarray(table) for table in tables(nx, ny))
    in_specs = (P(None, "gx", "gy", None), P("gx", "gy", None), P(None, "gx", "gy", None))
    out_specs = (P(None, "gx", "gy", None), P(None, "gx", "gy", None))
    return jax.shard_map(
        functools.partial(local, nx, ny, constants),
        mesh=mesh, in_specs=in_specs, out_specs=out_specs, check_vma=False,
    )
```

```python
import functools
import math

import jax
import jax.numpy as jnp
import numpy as np
from jax import lax
from jax.experimental import pallas as pl
from jax.experimental.pallas import tpu as pltpu
from jax.sharding import PartitionSpec as P

MESH = pl.DeviceIdType.MESH
NZ = 128
STEPS = 4
CUT = 4
VELOCITY = [
    (0, 0, 0),
    (1, 0, 0),
    (-1, 0, 0),
    (0, 1, 0),
    (0, -1, 0),
    (0, 0, 1),
    (0, 0, -1),
    (1, 1, 0),
    (-1, -1, 0),
    (1, -1, 0),
    (-1, 1, 0),
    (1, 0, 1),
    (-1, 0, -1),
    (1, 0, -1),
    (-1, 0, 1),
    (0, 1, 1),
    (0, -1, -1),
    (0, 1, -1),
    (0, -1, 1),
]
WEIGHTS = [1.0 / 3.0] + [1.0 / 18.0] * 6 + [1.0 / 36.0] * 12
SLOW_VISCOSITY = 0.0004
PAIRS = [(0, 0), (1, 1), (2, 2), (0, 1), (0, 2), (1, 2)]
EVEN = 4
CROSS = {
    (axis, sign): [i for i in range(19) if VELOCITY[i][axis] == sign] for axis in (0, 1) for sign in (1, -1)
}
MESSAGES = 8


def wave_table(length):
    index = np.arange(length)
    return 2.0 * np.pi * np.where(index >= (length + 1) // 2, index - length, index) / length


def response(nx, ny, nz):
    waves = np.meshgrid(wave_table(nx), wave_table(ny), wave_table(nz), indexing="ij")
    square = waves[0] ** 2 + waves[1] ** 2 + waves[2] ** 2
    safe = np.where(square > 0, square, 1.0)
    out = np.zeros((3, 6, nx, ny, nz // 2 + 1), np.complex128)
    for c, (p, q) in enumerate(PAIRS):
        force = [np.zeros_like(square) for _ in range(3)]
        force[p] = force[p] + waves[q]
        if p != q:
            force[q] = force[q] + waves[p]
        inner = sum(waves[a] * force[a] for a in range(3))
        for a in range(3):
            gain = np.where(square > 0, (force[a] - waves[a] * inner / safe) / (SLOW_VISCOSITY * safe), 0.0)
            mirror = np.roll(gain[::-1, ::-1, ::-1], (1, 1, 1), (0, 1, 2))
            odd = 0.5 * (gain - mirror)
            out[a, c] = np.fft.ifft2(-1j * odd, axes=(0, 1))[:, :, : nz // 2 + 1]
    return out


def tables(nx, ny):
    slow = NZ // CUT
    half = slow // 2
    green = response(nx, 2 * ny, slow)
    count = nx * ny
    send = np.zeros((count, 12, 2, 4, slow))
    place = {(0, 0): (0, 0), (0, 1): (0, 1), (2, 0): (0, 2), (2, 1): (0, 3), (1, 0): (1, 0), (1, 1): (1, 1)}
    far_x = np.arange(count) // ny
    far_y = np.arange(count) % ny
    for c in range(6):
        for half_y in range(2):
            for (a, to_y), (row, block) in place.items():
                g = green[a, c][far_x, (2 * far_y + to_y - half_y) % (2 * ny)]
                inside = g[:, 1:half]
                if a < 2:
                    inside = inside.real if c < EVEN else inside.imag
                else:
                    inside = inside.imag if c < EVEN else -inside.real
                send[:, 2 * c + half_y, row, block, : half + 1] = g.real
                send[:, 2 * c + half_y, row, block, 1:half] = inside
                send[:, 2 * c + half_y, row, block, half + 1 :] = inside
    send = send.reshape(count // 4, 4, 12, 2, NZ).transpose(0, 2, 1, 3, 4).reshape(count // 4, 12, 8, NZ)
    place_z = np.arange(slow)
    angle = 2.0 * np.pi * place_z[:, None] * np.arange(half + 1)[None, :] / slow
    cosine, sine = np.cos(angle), np.sin(angle)
    plain = np.concatenate([cosine, -sine[:, 1:half]], axis=1)
    turned = np.concatenate([cosine[:, :1], sine[:, 1:half], cosine[:, half:], cosine[:, 1:half]], axis=1)
    scale = 1.0 / (STEPS * CUT**3)
    forward = np.concatenate([np.tile(plain, (CUT, 1, 4)).reshape(CUT, slow, NZ).transpose(1, 0, 2).reshape(NZ, NZ),
                              np.tile(turned, (CUT, 1, 4)).reshape(CUT, slow, NZ).transpose(1, 0, 2).reshape(NZ, NZ)], axis=1)
    forward = forward * scale
    edge = [cosine[:, :1], cosine[:, half:]]
    back = np.concatenate([edge[0], 2 * cosine[:, 1:half], edge[1], -2 * sine[:, 1:half]], axis=1).T / slow
    back_turned = np.concatenate([edge[0], -2 * sine[:, 1:half], edge[1], -2 * cosine[:, 1:half]], axis=1).T / slow
    inverse = np.concatenate([back, back, back_turned, back_turned], axis=0)
    inverse = np.concatenate([inverse, np.zeros((NZ, NZ - slow))], axis=1)
    return send.astype(np.float32), forward.astype(np.float32), inverse.astype(np.float32)


def dot(left, right):
    return jnp.dot(left, right, precision=lax.Precision.HIGHEST, preferred_element_type=jnp.float32)


def moments(f):
    rho = f[0]
    for i in range(1, 19):
        rho = rho + f[i]
    j = []
    for axis in range(3):
        plus = [f[i] for i in range(19) if VELOCITY[i][axis] == 1]
        minus = [f[i] for i in range(19) if VELOCITY[i][axis] == -1]
        total = plus[0] - minus[0]
        for one, other in zip(plus[1:], minus[1:]):
            total = total + (one - other)
        j.append(total)
    return rho, j


def collide(f, rho, j, inverse, keep, omega, push, solid):
    speed = [one * inverse for one in j]
    square = speed[0] * speed[0] + speed[1] * speed[1] + speed[2] * speed[2]
    weight = omega * rho
    base = weight * (1.0 - 1.5 * square)
    quad = 4.5 * weight
    lead = [3.0 * (omega * j[a] + push[a]) for a in range(3)]
    post = [None] * 19
    post[0] = jnp.where(solid, f[0], keep * f[0] + WEIGHTS[0] * base)
    for i in range(1, 19, 2):
        along = linear = None
        for axis in range(3):
            c = VELOCITY[i][axis]
            if c:
                along = c * speed[axis] if along is None else along + speed[axis] if c > 0 else along - speed[axis]
                linear = c * lead[axis] if linear is None else linear + lead[axis] if c > 0 else linear - lead[axis]
        even = WEIGHTS[i] * (base + quad * (along * along))
        odd = WEIGHTS[i] * linear
        post[i] = jnp.where(solid, f[i + 1], keep * f[i] + (even + odd))
        post[i + 1] = jnp.where(solid, f[i], keep * f[i + 1] + (even - odd))
    return post


def kernel(
    nx, ny, pops_hbm, label_hbm, drive_hbm, table_hbm, forward_hbm, inverse_hbm, momentum_hbm, running_ref,
    state, label, drive, table, forward, inverse_z, momentum, face_out, face_in, row_out, row_in, edge_out, edge_in,
    message, arrived, load_sem, const_sem, halo_send, halo_recv, slow_send, slow_recv, out_sem,
):
    width = label.shape[0]
    gx = lax.axis_index("gx")
    gy = lax.axis_index("gy")
    count = nx * ny

    loads = [
        pltpu.make_async_copy(pops_hbm, state.at[0], load_sem.at[0]),
        pltpu.make_async_copy(label_hbm, label, load_sem.at[1]),
        pltpu.make_async_copy(drive_hbm, drive, load_sem.at[2]),
    ]
    constants = [
        pltpu.make_async_copy(table_hbm, table, const_sem.at[0]),
        pltpu.make_async_copy(forward_hbm, forward, const_sem.at[1]),
        pltpu.make_async_copy(inverse_hbm, inverse_z, const_sem.at[2]),
    ]
    for copy in loads + constants:
        copy.start()

    def device_at(far):
        return (lax.rem(gx + far // ny, nx), lax.rem(gy + far % ny, ny))

    def over_others(body):
        if count <= 64:
            for far in range(1, count):
                body(far)
        else:
            def step(far, carry):
                body(far)
                return carry

            lax.fori_loop(1, count, step, 0)

    barrier = pltpu.get_barrier_semaphore()
    over_others(lambda far: pl.semaphore_signal(barrier, inc=1, device_id=device_at(far), device_id_type=MESH))

    for copy in loads:
        copy.wait()

    east, west = lax.rem(gx + 1, nx), lax.rem(gx + nx - 1, nx)
    north, south = lax.rem(gy + 1, ny), lax.rem(gy + ny - 1, ny)
    side_x = {1: east, -1: west}
    side_y = {1: north, -1: south}
    slot = {1: 0, -1: 1}

    def remote(src, dst, step, number, place):
        return pltpu.make_async_remote_copy(
            src_ref=src,
            dst_ref=dst,
            send_sem=halo_send.at[step, number],
            recv_sem=halo_recv.at[step, number],
            device_id=place,
            device_id_type=MESH,
        )

    def halo(step):
        faces, rows = [], []
        for sign in (1, -1):
            s = slot[sign]
            faces.append(remote(face_out.at[step, s], face_in.at[step, s], step, s, (side_x[sign], gy)))
        if ny == 2:
            for sign in (1, -1):
                s = slot[sign]
                faces.append(remote(edge_out.at[step, s], edge_in.at[step, s], step, 4 + s, (side_x[sign], north)))
            rows.append(remote(row_out.at[step], row_in.at[step], step, 2, (gx, north)))
        else:
            for sign in (1, -1):
                s = slot[sign]
                for turn in (1, -1):
                    t = slot[turn]
                    faces.append(
                        remote(
                            edge_out.at[step, t, s], edge_in.at[step, t, s], step, 4 + 2 * t + s,
                            (side_x[turn], side_y[sign]),
                        )
                    )
                rows.append(remote(row_out.at[step, s], row_in.at[step, s], step, 2 + s, (gx, side_y[sign])))
        return faces, rows

    row_id = lax.broadcasted_iota(jnp.int32, (8, NZ), 0)
    first_row = row_id == 0
    last_row = row_id == 7

    def read(step, i, p):
        cx, cy, _ = VELOCITY[i]
        if step == 0:
            return state[0, i, p]
        outside = (cx == 1 and p == 0) or (cx == -1 and p == width - 1)
        if outside:
            value = face_in[step - 1, slot[cx], CROSS[0, cx].index(i)]
        else:
            value = state[step % 2, i, p]
        if cy:
            if outside:
                row = edge_in[step - 1, slot[cx], slot[cy]]
            else:
                row = row_in[step - 1, slot[cy], CROSS[1, cy].index(i) * width + p]
            value = jnp.where(first_row if cy == 1 else last_row, jnp.broadcast_to(row, (8, NZ)), value)
        return value

    def write(step, i, p, value):
        cx, cy, cz = VELOCITY[i]
        if cz:
            value = pltpu.roll(value, cz % NZ, 1)
        if cy:
            value = pltpu.roll(value, cy % 8, 0)
            line = value[0:1] if cy == 1 else value[7:8]
        outside = (cx == 1 and p == width - 1) or (cx == -1 and p == 0)
        if outside:
            face_out[step, slot[cx], CROSS[0, cx].index(i)] = value
            if cy:
                edge_out[step, slot[cx], slot[cy]] = line
        else:
            state[(step + 1) % 2, i, p + cx] = value
            if cy:
                row_out[step, slot[cy], CROSS[1, cy].index(i) * width + p + cx] = line

    def send_copy(far):
        return pltpu.make_async_remote_copy(
            src_ref=message.at[far],
            dst_ref=arrived.at[far],
            send_sem=slow_send,
            recv_sem=slow_recv,
            device_id=device_at(far),
            device_id_type=MESH,
        )

    total = [None] * 6

    def advance(step, p):
        phase = math.cos(2.0 * math.pi * (step + 0.5) / STEPS)
        f = [read(step, i, p) for i in range(19)]
        rho, j = moments(f)
        inverse = 1.0 / rho
        kind = label[p]
        solid = kind == 2
        thin = jnp.where(solid, 0.0, inverse)
        scaled = [one * thin for one in j]
        for c, (a, b) in enumerate(PAIRS):
            term = scaled[a] * j[b]
            total[c] = term if total[c] is None else total[c] + term
        second = kind == 1
        omega = jnp.where(second, 1.1, 1.6)
        strength = jnp.where(second, 0.6 * phase, phase)
        push = [strength * drive[a, p] for a in range(3)]
        post = collide(f, rho, j, inverse, 1.0 - omega, omega, push, solid)
        for i in range(19):
            write(step, i, p, post[i])

    outer = [0, width - 1]
    inner = list(range(1, width - 1))
    started = []
    for step in range(STEPS):
        if step == 0:
            for p in outer:
                advance(step, p)
            pl.semaphore_wait(barrier, count - 1)
        else:
            for copy in rows:
                copy.wait_recv()
            for p in inner:
                advance(step, p)
            for copy in faces:
                copy.wait_recv()
            for p in outer:
                advance(step, p)
        faces, rows = halo(step)
        started += faces + rows
        for copy in faces:
            copy.start()
        if step == 0:
            for p in inner:
                advance(step, p)
        for copy in rows:
            copy.start()

    for copy in constants:
        copy.wait()
    plain = dot(jnp.concatenate(total[:EVEN], axis=0), forward[:, :NZ])
    turned = dot(jnp.concatenate(total[EVEN:], axis=0), forward[:, NZ:])
    lines = []
    for c in range(6):
        tile = plain[8 * c : 8 * c + 8] if c < EVEN else turned[8 * (c - EVEN) : 8 * (c - EVEN) + 8]
        tile = tile + pltpu.roll(tile, 7, 0)
        tile = tile + pltpu.roll(tile, 6, 0)
        lines.append(jnp.broadcast_to(tile[0:1], (8, NZ)))
        lines.append(jnp.broadcast_to(tile[4:5], (8, NZ)))

    def group(g):
        value = lines[0] * table[g, 0]
        for k in range(1, 12):
            value = value + lines[k] * table[g, k]
        for k in range(4):
            message[4 * g + k] = value[2 * k : 2 * k + 2]

    if count <= 64:
        for g in range(count // 4):
            group(g)
    else:
        def each(g, carry):
            group(g)
            return carry

        lax.fori_loop(0, count // 4, each, 0)
    over_others(lambda far: send_copy(far).start())

    for copy in faces + rows:
        copy.wait_recv()
    for p in range(width):
        f = [None] + [read(STEPS, i, p) for i in range(1, 19)]
        for axis in range(3):
            value = None
            for i in range(1, 19):
                c = VELOCITY[i][axis]
                if c:
                    value = c * f[i] if value is None else value + f[i] if c > 0 else value - f[i]
            momentum[axis, p] = value
    out_copy = pltpu.make_async_copy(momentum, momentum_hbm, out_sem)
    out_copy.start()
    for copy in started:
        copy.wait_send()

    rest = pl.ds(1, count - 1)
    pltpu.make_async_copy(message.at[rest], arrived.at[rest], slow_recv).wait()
    spectrum = message[0]
    if count <= 64:
        for far in range(1, count):
            spectrum = spectrum + arrived[far]
    else:
        spectrum = lax.fori_loop(1, count, lambda far, value: value + arrived[far], spectrum)
    upper = jnp.broadcast_to(spectrum[0:1], (8, NZ))
    lower = jnp.broadcast_to(spectrum[1:2], (8, NZ))
    lane = lax.broadcasted_iota(jnp.int32, (8, NZ), 1)
    slow_z = NZ // CUT
    block = row_id % 2 + jnp.where(row_id >= 4, 2, 0)
    low = slow_z * block
    spread = jnp.where((row_id == 2) | (row_id == 3), lower, upper)
    spread = jnp.where((lane >= low) & (lane < low + slow_z), spread, 0.0)
    result = dot(spread, inverse_z[...])
    for a in range(3):
        running_ref[a, 0] = result[2 * a : 2 * a + 2, :slow_z]
    pltpu.make_async_copy(arrived.at[rest], message.at[rest], slow_send).wait()
    out_copy.wait()


def local(nx, ny, constants, pops, label, drive):
    width, height = pops.shape[1], pops.shape[2]
    count = nx * ny
    send, forward, inverse = constants
    anywhere = pl.BlockSpec(memory_space=pltpu.HBM)
    f32 = jnp.float32
    return pl.pallas_call(
        functools.partial(kernel, nx, ny),
        out_shape=(
            jax.ShapeDtypeStruct((3, width, height, NZ), f32),
            jax.ShapeDtypeStruct((3, width // CUT, height // CUT, NZ // CUT), f32),
        ),
        in_specs=[anywhere] * 6,
        out_specs=(anywhere, pl.BlockSpec(memory_space=pltpu.VMEM)),
        scratch_shapes=[
            pltpu.VMEM((2, 19, width, height, NZ), f32),
            pltpu.VMEM((width, height, NZ), jnp.int32),
            pltpu.VMEM((3, width, height, NZ), f32),
            pltpu.VMEM(send.shape, f32),
            pltpu.VMEM(forward.shape, f32),
            pltpu.VMEM(inverse.shape, f32),
            pltpu.VMEM((3, width, height, NZ), f32),
            pltpu.VMEM((STEPS, 2, 5, height, NZ), f32),
            pltpu.VMEM((STEPS, 2, 5, height, NZ), f32),
            pltpu.VMEM((STEPS, 2, 5 * width, 1, NZ), f32),
            pltpu.VMEM((STEPS, 2, 5 * width, 1, NZ), f32),
            pltpu.VMEM((STEPS, 2, 2, 1, NZ), f32),
            pltpu.VMEM((STEPS, 2, 2, 1, NZ), f32),
            pltpu.VMEM((count, 2, NZ), f32),
            pltpu.VMEM((count, 2, NZ), f32),
            pltpu.SemaphoreType.DMA((3,)),
            pltpu.SemaphoreType.DMA((3,)),
            pltpu.SemaphoreType.DMA((STEPS, MESSAGES)),
            pltpu.SemaphoreType.DMA((STEPS, MESSAGES)),
            pltpu.SemaphoreType.DMA,
            pltpu.SemaphoreType.DMA,
            pltpu.SemaphoreType.DMA,
        ],
        compiler_params=pltpu.CompilerParams(
            collective_id=0, has_side_effects=True, vmem_limit_bytes=60 * 1024 * 1024
        ),
        name="cycle",
    )(pops, label, drive, send, forward, inverse)


def solution(mesh):
    nx, ny = mesh.shape["gx"], mesh.shape["gy"]
    constants = tuple(jnp.asarray(table) for table in tables(nx, ny))
    in_specs = (P(None, "gx", "gy", None), P("gx", "gy", None), P(None, "gx", "gy", None))
    out_specs = (P(None, "gx", "gy", None), P(None, "gx", "gy", None))
    return jax.shard_map(
        functools.partial(local, nx, ny, constants),
        mesh=mesh, in_specs=in_specs, out_specs=out_specs, check_vma=False,
    )
```

```python
import functools
import math

import jax
import jax.numpy as jnp
import numpy as np
from jax import lax
from jax.experimental import pallas as pl
from jax.experimental.pallas import tpu as pltpu
from jax.sharding import PartitionSpec as P

MESH = pl.DeviceIdType.MESH
NZ = 128
STEPS = 4
CUT = 4
VELOCITY = [
    (0, 0, 0),
    (1, 0, 0),
    (-1, 0, 0),
    (0, 1, 0),
    (0, -1, 0),
    (0, 0, 1),
    (0, 0, -1),
    (1, 1, 0),
    (-1, -1, 0),
    (1, -1, 0),
    (-1, 1, 0),
    (1, 0, 1),
    (-1, 0, -1),
    (1, 0, -1),
    (-1, 0, 1),
    (0, 1, 1),
    (0, -1, -1),
    (0, 1, -1),
    (0, -1, 1),
]
WEIGHTS = [1.0 / 3.0] + [1.0 / 18.0] * 6 + [1.0 / 36.0] * 12
SLOW_VISCOSITY = 0.0004
PAIRS = [(0, 0), (1, 1), (2, 2), (0, 1), (0, 2), (1, 2)]
EVEN = 4
CROSS = {
    (axis, sign): [i for i in range(19) if VELOCITY[i][axis] == sign] for axis in (0, 1) for sign in (1, -1)
}
MESSAGES = 8


def wave_table(length):
    index = np.arange(length)
    return 2.0 * np.pi * np.where(index >= (length + 1) // 2, index - length, index) / length


def response(nx, ny, nz):
    waves = np.meshgrid(wave_table(nx), wave_table(ny), wave_table(nz), indexing="ij")
    square = waves[0] ** 2 + waves[1] ** 2 + waves[2] ** 2
    safe = np.where(square > 0, square, 1.0)
    out = np.zeros((3, 6, nx, ny, nz // 2 + 1), np.complex128)
    for c, (p, q) in enumerate(PAIRS):
        force = [np.zeros_like(square) for _ in range(3)]
        force[p] = force[p] + waves[q]
        if p != q:
            force[q] = force[q] + waves[p]
        inner = sum(waves[a] * force[a] for a in range(3))
        for a in range(3):
            gain = np.where(square > 0, (force[a] - waves[a] * inner / safe) / (SLOW_VISCOSITY * safe), 0.0)
            mirror = np.roll(gain[::-1, ::-1, ::-1], (1, 1, 1), (0, 1, 2))
            odd = 0.5 * (gain - mirror)
            out[a, c] = np.fft.ifft2(-1j * odd, axes=(0, 1))[:, :, : nz // 2 + 1]
    return out


def tables(nx, ny):
    slow = NZ // CUT
    half = slow // 2
    green = response(nx, 2 * ny, slow)
    count = nx * ny
    send = np.zeros((count, 12, 2, 4, slow))
    place = {(0, 0): (0, 0), (0, 1): (0, 1), (2, 0): (0, 2), (2, 1): (0, 3), (1, 0): (1, 0), (1, 1): (1, 1)}
    far_x = np.arange(count) // ny
    far_y = np.arange(count) % ny
    for c in range(6):
        for half_y in range(2):
            for (a, to_y), (row, block) in place.items():
                g = green[a, c][far_x, (2 * far_y + to_y - half_y) % (2 * ny)]
                inside = g[:, 1:half]
                if a < 2:
                    inside = inside.real if c < EVEN else inside.imag
                else:
                    inside = inside.imag if c < EVEN else -inside.real
                send[:, 2 * c + half_y, row, block, : half + 1] = g.real
                send[:, 2 * c + half_y, row, block, 1:half] = inside
                send[:, 2 * c + half_y, row, block, half + 1 :] = inside
    send = send.reshape(count // 4, 4, 12, 2, NZ).transpose(0, 2, 1, 3, 4).reshape(count // 4, 12, 8, NZ)
    place_z = np.arange(slow)
    angle = 2.0 * np.pi * place_z[:, None] * np.arange(half + 1)[None, :] / slow
    cosine, sine = np.cos(angle), np.sin(angle)
    plain = np.concatenate([cosine, -sine[:, 1:half]], axis=1)
    turned = np.concatenate([cosine[:, :1], sine[:, 1:half], cosine[:, half:], cosine[:, 1:half]], axis=1)
    scale = 1.0 / (STEPS * CUT**3)
    forward = np.concatenate([np.tile(plain, (CUT, 1, 4)).reshape(CUT, slow, NZ).transpose(1, 0, 2).reshape(NZ, NZ),
                              np.tile(turned, (CUT, 1, 4)).reshape(CUT, slow, NZ).transpose(1, 0, 2).reshape(NZ, NZ)], axis=1)
    forward = forward * scale
    edge = [cosine[:, :1], cosine[:, half:]]
    back = np.concatenate([edge[0], 2 * cosine[:, 1:half], edge[1], -2 * sine[:, 1:half]], axis=1).T / slow
    back_turned = np.concatenate([edge[0], -2 * sine[:, 1:half], edge[1], -2 * cosine[:, 1:half]], axis=1).T / slow
    inverse = np.concatenate([back, back, back_turned, back_turned], axis=0)
    inverse = np.concatenate([inverse, np.zeros((NZ, NZ - slow))], axis=1)
    return send.astype(np.float32), forward.astype(np.float32), inverse.astype(np.float32)


def dot(left, right):
    return jnp.dot(left, right, precision=lax.Precision.HIGHEST, preferred_element_type=jnp.float32)


def moments(f):
    rho = f[0]
    for i in range(1, 19):
        rho = rho + f[i]
    j = []
    for axis in range(3):
        plus = [f[i] for i in range(19) if VELOCITY[i][axis] == 1]
        minus = [f[i] for i in range(19) if VELOCITY[i][axis] == -1]
        total = plus[0] - minus[0]
        for one, other in zip(plus[1:], minus[1:]):
            total = total + (one - other)
        j.append(total)
    return rho, j


def collide(f, rho, j, inverse, keep, omega, push, solid):
    speed = [one * inverse for one in j]
    square = speed[0] * speed[0] + speed[1] * speed[1] + speed[2] * speed[2]
    weight = omega * rho
    base = weight * (1.0 - 1.5 * square)
    quad = 4.5 * weight
    lead = [3.0 * (omega * j[a] + push[a]) for a in range(3)]
    post = [None] * 19
    post[0] = jnp.where(solid, f[0], keep * f[0] + WEIGHTS[0] * base)
    for i in range(1, 19, 2):
        along = linear = None
        for axis in range(3):
            c = VELOCITY[i][axis]
            if c:
                along = c * speed[axis] if along is None else along + speed[axis] if c > 0 else along - speed[axis]
                linear = c * lead[axis] if linear is None else linear + lead[axis] if c > 0 else linear - lead[axis]
        even = WEIGHTS[i] * (base + quad * (along * along))
        odd = WEIGHTS[i] * linear
        post[i] = jnp.where(solid, f[i + 1], keep * f[i] + (even + odd))
        post[i + 1] = jnp.where(solid, f[i], keep * f[i + 1] + (even - odd))
    return post


def kernel(
    nx, ny, pops_hbm, label_hbm, drive_hbm, table_hbm, forward_hbm, inverse_hbm, momentum_hbm, running_ref,
    state, stress, label, drive, table, forward, inverse_z, momentum, face_out, face_in, row_out, row_in, edge_out, edge_in,
    message, arrived, load_sem, const_sem, halo_send, halo_recv, slow_send, slow_recv, out_sem,
):
    width = label.shape[0]
    gx = lax.axis_index("gx")
    gy = lax.axis_index("gy")
    count = nx * ny

    loads = [
        pltpu.make_async_copy(pops_hbm, state.at[0], load_sem.at[0]),
        pltpu.make_async_copy(label_hbm, label, load_sem.at[1]),
        pltpu.make_async_copy(drive_hbm, drive, load_sem.at[2]),
    ]
    constants = [
        pltpu.make_async_copy(table_hbm, table, const_sem.at[0]),
        pltpu.make_async_copy(forward_hbm, forward, const_sem.at[1]),
        pltpu.make_async_copy(inverse_hbm, inverse_z, const_sem.at[2]),
    ]
    for copy in loads + constants:
        copy.start()

    def wrap(at, size):
        return jnp.where(at >= size, at - size, at)

    def over_others(body):
        for dy in range(1, ny):
            body(dy, (gx, wrap(gy + dy, ny)))

        def step(dx, carry):
            x = wrap(gx + dx, nx)
            for dy in range(ny):
                body(dx * ny + dy, (x, wrap(gy + dy, ny)))
            return carry

        lax.fori_loop(1, nx, step, 0)

    barrier = pltpu.get_barrier_semaphore()
    over_others(lambda far, place: pl.semaphore_signal(barrier, inc=1, device_id=place, device_id_type=MESH))
    for c in range(6):
        stress[c] = jnp.zeros((8, NZ), jnp.float32)

    for copy in loads:
        copy.wait()

    east, west = wrap(gx + 1, nx), wrap(gx + nx - 1, nx)
    north, south = wrap(gy + 1, ny), wrap(gy + ny - 1, ny)
    side_x = {1: east, -1: west}
    side_y = {1: north, -1: south}
    slot = {1: 0, -1: 1}

    def remote(src, dst, step, number, place):
        return pltpu.make_async_remote_copy(
            src_ref=src,
            dst_ref=dst,
            send_sem=halo_send.at[step, number],
            recv_sem=halo_recv.at[step, number],
            device_id=place,
            device_id_type=MESH,
        )

    def halo(step):
        faces, rows = [], []
        for sign in (1, -1):
            s = slot[sign]
            faces.append(remote(face_out.at[step, s], face_in.at[step + 1, s], step, s, (side_x[sign], gy)))
        if ny == 2:
            for sign in (1, -1):
                s = slot[sign]
                faces.append(remote(edge_out.at[step, s], edge_in.at[step + 1, s], step, 4 + s, (side_x[sign], north)))
            rows.append(remote(row_out.at[step], row_in.at[step + 1], step, 2, (gx, north)))
        else:
            for sign in (1, -1):
                s = slot[sign]
                for turn in (1, -1):
                    t = slot[turn]
                    faces.append(
                        remote(
                            edge_out.at[step, t, s], edge_in.at[step + 1, t, s], step, 4 + 2 * t + s,
                            (side_x[turn], side_y[sign]),
                        )
                    )
                rows.append(remote(row_out.at[step, s], row_in.at[step + 1, s], step, 2 + s, (gx, side_y[sign])))
        return faces, rows

    row_id = lax.broadcasted_iota(jnp.int32, (8, NZ), 0)

    def read(step, fresh, i, p):
        cx, cy, _ = VELOCITY[i]
        outside = (cx == 1 and p == 0) or (cx == -1 and p == width - 1)
        if outside:
            value = face_in[step, slot[cx], CROSS[0, cx].index(i)]
        else:
            value = state[step, i, p]
        if cy:
            if outside:
                row = edge_in[step, slot[cx], slot[cy]]
            else:
                row = row_in[step, slot[cy], CROSS[1, cy].index(i) * width + p]
            value = jnp.where(row_id == fresh[cy], jnp.broadcast_to(row, (8, NZ)), value)
        return value

    def write(step, i, p, value):
        cx, cy, cz = VELOCITY[i]
        if cz:
            value = pltpu.roll(value, cz % NZ, 1)
        if cy:
            value = pltpu.roll(value, cy % 8, 0)
            line = value[0:1] if cy == 1 else value[7:8]
        outside = (cx == 1 and p == width - 1) or (cx == -1 and p == 0)
        if outside:
            face_out[step, slot[cx], CROSS[0, cx].index(i)] = value
            if cy:
                edge_out[step, slot[cx], slot[cy]] = line
        else:
            state[step + 1, i, p + cx] = value
            if cy:
                row_out[step, slot[cy], CROSS[1, cy].index(i) * width + p + cx] = line

    def send_copy(far, place):
        return pltpu.make_async_remote_copy(
            src_ref=message.at[far],
            dst_ref=arrived.at[far],
            send_sem=slow_send,
            recv_sem=slow_recv,
            device_id=place,
            device_id_type=MESH,
        )

    def advance(step, planes):
        quarter = math.cos(math.pi / 4.0)
        phase = jnp.where((step == 0) | (step == STEPS - 1), quarter, -quarter)
        fresh = {1: jnp.where(step > 0, 0, -1), -1: jnp.where(step > 0, 7, -1)}
        total = [None] * 6
        for p in planes:
            f = [read(step, fresh, i, p) for i in range(19)]
            rho, j = moments(f)
            inverse = 1.0 / rho
            kind = label[p]
            solid = kind == 2
            thin = jnp.where(solid, 0.0, inverse)
            scaled = [one * thin for one in j]
            for c, (a, b) in enumerate(PAIRS):
                term = scaled[a] * j[b]
                total[c] = term if total[c] is None else total[c] + term
            second = kind == 1
            omega = jnp.where(second, 1.1, 1.6)
            strength = jnp.where(second, 0.6 * phase, phase)
            push = [strength * drive[a, p] for a in range(3)]
            post = collide(f, rho, j, inverse, 1.0 - omega, omega, push, solid)
            for i in range(19):
                write(step, i, p, post[i])
        for c in range(6):
            stress[c] += total[c]

    for sign in (1, -1):
        for k, i in enumerate(CROSS[0, sign]):
            face_in[0, slot[sign], k] = state[0, i, 0 if sign == 1 else width - 1]

    def cycle_step(step, carry):
        @pl.when(step > 0)
        def _():
            for copy in halo(step - 1)[1]:
                copy.wait_recv()

        advance(step, range(1, width - 1))

        @pl.when(step > 0)
        def _():
            for copy in halo(step - 1)[0]:
                copy.wait_recv()

        advance(step, [0, width - 1])

        @pl.when(step == 0)
        def _():
            pl.semaphore_wait(barrier, count - 1)

        faces, rows = halo(step)
        for copy in faces + rows:
            copy.start()
        return carry

    lax.fori_loop(0, STEPS, cycle_step, 0)
    faces, rows = halo(STEPS - 1)

    for copy in constants:
        copy.wait()
    plain = dot(stress[:EVEN].reshape(8 * EVEN, NZ), forward[:, :NZ])
    turned = dot(stress[EVEN:].reshape(8 * (6 - EVEN), NZ), forward[:, NZ:])
    lines = []
    for c in range(6):
        tile = plain[8 * c : 8 * c + 8] if c < EVEN else turned[8 * (c - EVEN) : 8 * (c - EVEN) + 8]
        tile = tile + pltpu.roll(tile, 7, 0)
        tile = tile + pltpu.roll(tile, 6, 0)
        lines.append(jnp.broadcast_to(tile[0:1], (8, NZ)))
        lines.append(jnp.broadcast_to(tile[4:5], (8, NZ)))

    def group(g):
        value = lines[0] * table[g, 0]
        for k in range(1, 12):
            value = value + lines[k] * table[g, k]
        for k in range(4):
            message[4 * g + k] = value[2 * k : 2 * k + 2]

    if count <= 64:
        for g in range(count // 4):
            group(g)
    else:
        def each(g, carry):
            group(g)
            return carry

        lax.fori_loop(0, count // 4, each, 0)
    over_others(lambda far, place: send_copy(far, place).start())

    for copy in faces + rows:
        copy.wait_recv()
    for p in range(width):
        f = [None] + [read(STEPS, {1: 0, -1: 7}, i, p) for i in range(1, 19)]
        for axis in range(3):
            value = None
            for i in range(1, 19):
                c = VELOCITY[i][axis]
                if c:
                    value = c * f[i] if value is None else value + f[i] if c > 0 else value - f[i]
            momentum[axis, p] = value
    out_copy = pltpu.make_async_copy(momentum, momentum_hbm, out_sem)
    out_copy.start()
    for step in range(STEPS):
        for copy in halo(step)[0] + halo(step)[1]:
            copy.wait_send()

    rest = pl.ds(1, count - 1)
    pltpu.make_async_copy(message.at[rest], arrived.at[rest], slow_recv).wait()
    spectrum = message[0]
    if count <= 64:
        for far in range(1, count):
            spectrum = spectrum + arrived[far]
    else:
        spectrum = lax.fori_loop(1, count, lambda far, value: value + arrived[far], spectrum)
    upper = jnp.broadcast_to(spectrum[0:1], (8, NZ))
    lower = jnp.broadcast_to(spectrum[1:2], (8, NZ))
    lane = lax.broadcasted_iota(jnp.int32, (8, NZ), 1)
    slow_z = NZ // CUT
    block = row_id % 2 + jnp.where(row_id >= 4, 2, 0)
    low = slow_z * block
    spread = jnp.where((row_id == 2) | (row_id == 3), lower, upper)
    spread = jnp.where((lane >= low) & (lane < low + slow_z), spread, 0.0)
    result = dot(spread, inverse_z[...])
    for a in range(3):
        running_ref[a, 0] = result[2 * a : 2 * a + 2, :slow_z]
    pltpu.make_async_copy(arrived.at[rest], message.at[rest], slow_send).wait()
    out_copy.wait()


def local(nx, ny, constants, pops, label, drive):
    width, height = pops.shape[1], pops.shape[2]
    count = nx * ny
    send, forward, inverse = constants
    anywhere = pl.BlockSpec(memory_space=pltpu.HBM)
    f32 = jnp.float32
    return pl.pallas_call(
        functools.partial(kernel, nx, ny),
        out_shape=(
            jax.ShapeDtypeStruct((3, width, height, NZ), f32),
            jax.ShapeDtypeStruct((3, width // CUT, height // CUT, NZ // CUT), f32),
        ),
        in_specs=[anywhere] * 6,
        out_specs=(anywhere, pl.BlockSpec(memory_space=pltpu.VMEM)),
        scratch_shapes=[
            pltpu.VMEM((STEPS + 1, 19, width, height, NZ), f32),
            pltpu.VMEM((6, height, NZ), f32),
            pltpu.VMEM((width, height, NZ), jnp.int32),
            pltpu.VMEM((3, width, height, NZ), f32),
            pltpu.VMEM(send.shape, f32),
            pltpu.VMEM(forward.shape, f32),
            pltpu.VMEM(inverse.shape, f32),
            pltpu.VMEM((3, width, height, NZ), f32),
            pltpu.VMEM((STEPS, 2, 5, height, NZ), f32),
            pltpu.VMEM((STEPS + 1, 2, 5, height, NZ), f32),
            pltpu.VMEM((STEPS, 2, 5 * width, 1, NZ), f32),
            pltpu.VMEM((STEPS + 1, 2, 5 * width, 1, NZ), f32),
            pltpu.VMEM((STEPS, 2, 2, 1, NZ), f32),
            pltpu.VMEM((STEPS + 1, 2, 2, 1, NZ), f32),
            pltpu.VMEM((count, 2, NZ), f32),
            pltpu.VMEM((count, 2, NZ), f32),
            pltpu.SemaphoreType.DMA((3,)),
            pltpu.SemaphoreType.DMA((3,)),
            pltpu.SemaphoreType.DMA((STEPS, MESSAGES)),
            pltpu.SemaphoreType.DMA((STEPS, MESSAGES)),
            pltpu.SemaphoreType.DMA,
            pltpu.SemaphoreType.DMA,
            pltpu.SemaphoreType.DMA,
        ],
        compiler_params=pltpu.CompilerParams(
            collective_id=0, has_side_effects=True, vmem_limit_bytes=60 * 1024 * 1024
        ),
        name="cycle",
    )(pops, label, drive, send, forward, inverse)


def solution(mesh):
    nx, ny = mesh.shape["gx"], mesh.shape["gy"]
    constants = tuple(jnp.asarray(table) for table in tables(nx, ny))
    in_specs = (P(None, "gx", "gy", None), P("gx", "gy", None), P(None, "gx", "gy", None))
    out_specs = (P(None, "gx", "gy", None), P(None, "gx", "gy", None))
    return jax.shard_map(
        functools.partial(local, nx, ny, constants),
        mesh=mesh, in_specs=in_specs, out_specs=out_specs, check_vma=False,
    )
```

```python
import functools
import math

import jax
import jax.numpy as jnp
import numpy as np
from jax import lax
from jax.experimental import pallas as pl
from jax.experimental.pallas import tpu as pltpu
from jax.sharding import PartitionSpec as P

MESH = pl.DeviceIdType.MESH
NZ = 128
STEPS = 4
CUT = 4
VELOCITY = [
    (0, 0, 0),
    (1, 0, 0),
    (-1, 0, 0),
    (0, 1, 0),
    (0, -1, 0),
    (0, 0, 1),
    (0, 0, -1),
    (1, 1, 0),
    (-1, -1, 0),
    (1, -1, 0),
    (-1, 1, 0),
    (1, 0, 1),
    (-1, 0, -1),
    (1, 0, -1),
    (-1, 0, 1),
    (0, 1, 1),
    (0, -1, -1),
    (0, 1, -1),
    (0, -1, 1),
]
WEIGHTS = [1.0 / 3.0] + [1.0 / 18.0] * 6 + [1.0 / 36.0] * 12
SLOW_VISCOSITY = 0.0004
PAIRS = [(0, 0), (1, 1), (2, 2), (0, 1), (0, 2), (1, 2)]
EVEN = 4
CROSS = {
    (axis, sign): [i for i in range(19) if VELOCITY[i][axis] == sign] for axis in (0, 1) for sign in (1, -1)
}
MESSAGES = 8


def wave_table(length):
    index = np.arange(length)
    return 2.0 * np.pi * np.where(index >= (length + 1) // 2, index - length, index) / length


def response(nx, ny, nz):
    waves = np.meshgrid(wave_table(nx), wave_table(ny), wave_table(nz), indexing="ij")
    square = waves[0] ** 2 + waves[1] ** 2 + waves[2] ** 2
    safe = np.where(square > 0, square, 1.0)
    out = np.zeros((3, 6, nx, ny, nz // 2 + 1), np.complex128)
    for c, (p, q) in enumerate(PAIRS):
        force = [np.zeros_like(square) for _ in range(3)]
        force[p] = force[p] + waves[q]
        if p != q:
            force[q] = force[q] + waves[p]
        inner = sum(waves[a] * force[a] for a in range(3))
        for a in range(3):
            gain = np.where(square > 0, (force[a] - waves[a] * inner / safe) / (SLOW_VISCOSITY * safe), 0.0)
            mirror = np.roll(gain[::-1, ::-1, ::-1], (1, 1, 1), (0, 1, 2))
            odd = 0.5 * (gain - mirror)
            out[a, c] = np.fft.ifft2(-1j * odd, axes=(0, 1))[:, :, : nz // 2 + 1]
    return out


def tables(nx, ny):
    slow = NZ // CUT
    half = slow // 2
    green = response(nx, 2 * ny, slow)
    count = nx * ny
    send = np.zeros((count, 12, 2, 4, slow))
    place = {(0, 0): (0, 0), (0, 1): (0, 1), (2, 0): (0, 2), (2, 1): (0, 3), (1, 0): (1, 0), (1, 1): (1, 1)}
    far_x = np.arange(count) // ny
    far_y = np.arange(count) % ny
    for c in range(6):
        for half_y in range(2):
            for (a, to_y), (row, block) in place.items():
                g = green[a, c][far_x, (2 * far_y + to_y - half_y) % (2 * ny)]
                inside = g[:, 1:half]
                if a < 2:
                    inside = inside.real if c < EVEN else inside.imag
                else:
                    inside = inside.imag if c < EVEN else -inside.real
                send[:, 2 * c + half_y, row, block, : half + 1] = g.real
                send[:, 2 * c + half_y, row, block, 1:half] = inside
                send[:, 2 * c + half_y, row, block, half + 1 :] = inside
    send = send.reshape(count // 4, 4, 12, 2, NZ).transpose(0, 2, 1, 3, 4).reshape(count // 4, 12, 8, NZ)
    place_z = np.arange(slow)
    angle = 2.0 * np.pi * place_z[:, None] * np.arange(half + 1)[None, :] / slow
    cosine, sine = np.cos(angle), np.sin(angle)
    plain = np.concatenate([cosine, -sine[:, 1:half]], axis=1)
    turned = np.concatenate([cosine[:, :1], sine[:, 1:half], cosine[:, half:], cosine[:, 1:half]], axis=1)
    scale = 1.0 / (STEPS * CUT**3)
    forward = np.concatenate([np.tile(plain, (CUT, 1, 4)).reshape(CUT, slow, NZ).transpose(1, 0, 2).reshape(NZ, NZ),
                              np.tile(turned, (CUT, 1, 4)).reshape(CUT, slow, NZ).transpose(1, 0, 2).reshape(NZ, NZ)], axis=1)
    forward = forward * scale
    edge = [cosine[:, :1], cosine[:, half:]]
    back = np.concatenate([edge[0], 2 * cosine[:, 1:half], edge[1], -2 * sine[:, 1:half]], axis=1).T / slow
    back_turned = np.concatenate([edge[0], -2 * sine[:, 1:half], edge[1], -2 * cosine[:, 1:half]], axis=1).T / slow
    inverse = np.concatenate([back, back, back_turned, back_turned], axis=0)
    inverse = np.concatenate([inverse, np.zeros((NZ, NZ - slow))], axis=1)
    return send.astype(np.float32), forward.astype(np.float32), inverse.astype(np.float32)


def dot(left, right):
    return jnp.dot(left, right, precision=lax.Precision.HIGHEST, preferred_element_type=jnp.float32)


def moments(f):
    rho = f[0]
    for i in range(1, 19):
        rho = rho + f[i]
    j = []
    for axis in range(3):
        plus = [f[i] for i in range(19) if VELOCITY[i][axis] == 1]
        minus = [f[i] for i in range(19) if VELOCITY[i][axis] == -1]
        total = plus[0] - minus[0]
        for one, other in zip(plus[1:], minus[1:]):
            total = total + (one - other)
        j.append(total)
    return rho, j


def collide(f, rho, j, inverse, keep, omega, push, solid):
    speed = [one * inverse for one in j]
    square = speed[0] * speed[0] + speed[1] * speed[1] + speed[2] * speed[2]
    weight = omega * rho
    base = weight * (1.0 - 1.5 * square)
    quad = 4.5 * weight
    lead = [3.0 * (omega * j[a] + push[a]) for a in range(3)]
    post = [None] * 19
    post[0] = jnp.where(solid, f[0], keep * f[0] + WEIGHTS[0] * base)
    for i in range(1, 19, 2):
        along = linear = None
        for axis in range(3):
            c = VELOCITY[i][axis]
            if c:
                along = c * speed[axis] if along is None else along + speed[axis] if c > 0 else along - speed[axis]
                linear = c * lead[axis] if linear is None else linear + lead[axis] if c > 0 else linear - lead[axis]
        even = WEIGHTS[i] * (base + quad * (along * along))
        odd = WEIGHTS[i] * linear
        post[i] = jnp.where(solid, f[i + 1], keep * f[i] + (even + odd))
        post[i + 1] = jnp.where(solid, f[i], keep * f[i + 1] + (even - odd))
    return post


def kernel(
    nx, ny, pops_hbm, label_hbm, drive_hbm, table_hbm, forward_hbm, inverse_hbm, momentum, running_ref,
    state, stress, label, drive, table, forward, inverse_z, face_out, face_in, row_out, row_in, edge_out, edge_in,
    message, arrived, load_sem, const_sem, halo_send, halo_recv, slow_send, slow_recv,
):
    width = label.shape[0]
    gx = lax.axis_index("gx")
    gy = lax.axis_index("gy")
    count = nx * ny

    loads = [
        pltpu.make_async_copy(pops_hbm, state.at[0], load_sem.at[0]),
        pltpu.make_async_copy(label_hbm, label, load_sem.at[1]),
        pltpu.make_async_copy(drive_hbm, drive, load_sem.at[2]),
    ]
    constants = [
        pltpu.make_async_copy(table_hbm, table, const_sem.at[0]),
        pltpu.make_async_copy(forward_hbm, forward, const_sem.at[1]),
        pltpu.make_async_copy(inverse_hbm, inverse_z, const_sem.at[2]),
    ]
    for copy in loads + constants:
        copy.start()

    def wrap(at, size):
        return jnp.where(at >= size, at - size, at)

    def over_others(body):
        for dy in range(1, ny):
            body(dy, (gx, wrap(gy + dy, ny)))

        def step(dx, carry):
            x = wrap(gx + dx, nx)
            for dy in range(ny):
                body(dx * ny + dy, (x, wrap(gy + dy, ny)))
            return carry

        lax.fori_loop(1, nx, step, 0)

    barrier = pltpu.get_barrier_semaphore()
    over_others(lambda far, place: pl.semaphore_signal(barrier, inc=1, device_id=place, device_id_type=MESH))
    for c in range(6):
        stress[c] = jnp.zeros((8, NZ), jnp.float32)

    for copy in loads:
        copy.wait()

    east, west = wrap(gx + 1, nx), wrap(gx + nx - 1, nx)
    north, south = wrap(gy + 1, ny), wrap(gy + ny - 1, ny)
    side_x = {1: east, -1: west}
    side_y = {1: north, -1: south}
    slot = {1: 0, -1: 1}

    def remote(src, dst, step, number, place):
        return pltpu.make_async_remote_copy(
            src_ref=src,
            dst_ref=dst,
            send_sem=halo_send.at[step, number],
            recv_sem=halo_recv.at[step, number],
            device_id=place,
            device_id_type=MESH,
        )

    def halo(step):
        faces, rows = [], []
        for sign in (1, -1):
            s = slot[sign]
            faces.append(remote(face_out.at[step, s], face_in.at[step + 1, s], step, s, (side_x[sign], gy)))
        if ny == 2:
            for sign in (1, -1):
                s = slot[sign]
                faces.append(remote(edge_out.at[step, s], edge_in.at[step + 1, s], step, 4 + s, (side_x[sign], north)))
            rows.append(remote(row_out.at[step], row_in.at[step + 1], step, 2, (gx, north)))
        else:
            for sign in (1, -1):
                s = slot[sign]
                for turn in (1, -1):
                    t = slot[turn]
                    faces.append(
                        remote(
                            edge_out.at[step, t, s], edge_in.at[step + 1, t, s], step, 4 + 2 * t + s,
                            (side_x[turn], side_y[sign]),
                        )
                    )
                rows.append(remote(row_out.at[step, s], row_in.at[step + 1, s], step, 2 + s, (gx, side_y[sign])))
        return faces, rows

    row_id = lax.broadcasted_iota(jnp.int32, (8, NZ), 0)

    def read(step, fresh, i, p):
        cx, cy, _ = VELOCITY[i]
        outside = (cx == 1 and p == 0) or (cx == -1 and p == width - 1)
        if outside:
            value = face_in[step, slot[cx], CROSS[0, cx].index(i)]
        else:
            value = state[step, i, p]
        if cy:
            if outside:
                row = edge_in[step, slot[cx], slot[cy]]
            else:
                row = row_in[step, slot[cy], CROSS[1, cy].index(i) * width + p]
            value = jnp.where(row_id == fresh[cy], jnp.broadcast_to(row, (8, NZ)), value)
        return value

    def write(step, i, p, value):
        cx, cy, cz = VELOCITY[i]
        if cz:
            value = pltpu.roll(value, cz % NZ, 1)
        if cy:
            value = pltpu.roll(value, cy % 8, 0)
            line = value[0:1] if cy == 1 else value[7:8]
        outside = (cx == 1 and p == width - 1) or (cx == -1 and p == 0)
        if outside:
            face_out[step, slot[cx], CROSS[0, cx].index(i)] = value
            if cy:
                edge_out[step, slot[cx], slot[cy]] = line
        else:
            state[step + 1, i, p + cx] = value
            if cy:
                row_out[step, slot[cy], CROSS[1, cy].index(i) * width + p + cx] = line

    def send_copy(far, place):
        return pltpu.make_async_remote_copy(
            src_ref=message.at[far],
            dst_ref=arrived.at[far],
            send_sem=slow_send,
            recv_sem=slow_recv,
            device_id=place,
            device_id_type=MESH,
        )

    def advance(step, planes):
        quarter = math.cos(math.pi / 4.0)
        phase = jnp.where((step == 0) | (step == STEPS - 1), quarter, -quarter)
        fresh = {1: jnp.where(step > 0, 0, -1), -1: jnp.where(step > 0, 7, -1)}
        total = [None] * 6
        for p in planes:
            f = [read(step, fresh, i, p) for i in range(19)]
            rho, j = moments(f)
            inverse = 1.0 / rho
            kind = label[p]
            solid = kind == 2
            thin = jnp.where(solid, 0.0, inverse)
            scaled = [one * thin for one in j]
            for c, (a, b) in enumerate(PAIRS):
                term = scaled[a] * j[b]
                total[c] = term if total[c] is None else total[c] + term
            second = kind == 1
            omega = jnp.where(second, 1.1, 1.6)
            strength = jnp.where(second, 0.6 * phase, phase)
            push = [strength * drive[a, p] for a in range(3)]
            post = collide(f, rho, j, inverse, 1.0 - omega, omega, push, solid)
            for i in range(19):
                write(step, i, p, post[i])
        for c in range(6):
            stress[c] += total[c]

    for sign in (1, -1):
        for k, i in enumerate(CROSS[0, sign]):
            face_in[0, slot[sign], k] = state[0, i, 0 if sign == 1 else width - 1]

    def cycle_step(step, carry):
        @pl.when(step > 0)
        def _():
            for copy in halo(step - 1)[1]:
                copy.wait_recv()

        advance(step, range(1, width - 1))

        @pl.when(step > 0)
        def _():
            for copy in halo(step - 1)[0]:
                copy.wait_recv()

        advance(step, [0, width - 1])

        @pl.when(step == 0)
        def _():
            pl.semaphore_wait(barrier, count - 1)

        faces, rows = halo(step)
        for copy in faces + rows:
            copy.start()
        return carry

    lax.fori_loop(0, STEPS, cycle_step, 0)
    faces, rows = halo(STEPS - 1)

    for copy in constants:
        copy.wait()
    plain = dot(stress[:EVEN].reshape(8 * EVEN, NZ), forward[:, :NZ])
    turned = dot(stress[EVEN:].reshape(8 * (6 - EVEN), NZ), forward[:, NZ:])
    lines = []
    for c in range(6):
        tile = plain[8 * c : 8 * c + 8] if c < EVEN else turned[8 * (c - EVEN) : 8 * (c - EVEN) + 8]
        tile = tile + pltpu.roll(tile, 7, 0)
        tile = tile + pltpu.roll(tile, 6, 0)
        lines.append(jnp.broadcast_to(tile[0:1], (8, NZ)))
        lines.append(jnp.broadcast_to(tile[4:5], (8, NZ)))

    def group(g):
        value = lines[0] * table[g, 0]
        for k in range(1, 12):
            value = value + lines[k] * table[g, k]
        for k in range(4):
            message[4 * g + k] = value[2 * k : 2 * k + 2]

    if count <= 64:
        for g in range(count // 4):
            group(g)
    else:
        def each(g, carry):
            group(g)
            return carry

        lax.fori_loop(0, count // 4, each, 0)
    over_others(lambda far, place: send_copy(far, place).start())

    for copy in faces + rows:
        copy.wait_recv()
    for p in range(width):
        f = [None] + [read(STEPS, {1: 0, -1: 7}, i, p) for i in range(1, 19)]
        for axis in range(3):
            value = None
            for i in range(1, 19):
                c = VELOCITY[i][axis]
                if c:
                    value = c * f[i] if value is None else value + f[i] if c > 0 else value - f[i]
            momentum[axis, p] = value
    for step in range(STEPS):
        for copy in halo(step)[0] + halo(step)[1]:
            copy.wait_send()

    rest = pl.ds(1, count - 1)
    pltpu.make_async_copy(message.at[rest], arrived.at[rest], slow_recv).wait()
    spectrum = message[0]
    if count <= 64:
        for far in range(1, count):
            spectrum = spectrum + arrived[far]
    else:
        spectrum = lax.fori_loop(1, count, lambda far, value: value + arrived[far], spectrum)
    upper = jnp.broadcast_to(spectrum[0:1], (8, NZ))
    lower = jnp.broadcast_to(spectrum[1:2], (8, NZ))
    lane = lax.broadcasted_iota(jnp.int32, (8, NZ), 1)
    slow_z = NZ // CUT
    block = row_id % 2 + jnp.where(row_id >= 4, 2, 0)
    low = slow_z * block
    spread = jnp.where((row_id == 2) | (row_id == 3), lower, upper)
    spread = jnp.where((lane >= low) & (lane < low + slow_z), spread, 0.0)
    result = dot(spread, inverse_z[...])
    for a in range(3):
        running_ref[a, 0] = result[2 * a : 2 * a + 2, :slow_z]
    pltpu.make_async_copy(arrived.at[rest], message.at[rest], slow_send).wait()


def local(nx, ny, constants, pops, label, drive):
    width, height = pops.shape[1], pops.shape[2]
    count = nx * ny
    send, forward, inverse = constants
    anywhere = pl.BlockSpec(memory_space=pltpu.HBM)
    f32 = jnp.float32
    return pl.pallas_call(
        functools.partial(kernel, nx, ny),
        out_shape=(
            pltpu.VMEM((3, width, height, NZ), f32),
            pltpu.VMEM((3, width // CUT, height // CUT, NZ // CUT), f32),
        ),
        in_specs=[anywhere] * 6,
        out_specs=(pl.BlockSpec(memory_space=pltpu.VMEM),) * 2,
        scratch_shapes=[
            pltpu.VMEM((STEPS + 1, 19, width, height, NZ), f32),
            pltpu.VMEM((6, height, NZ), f32),
            pltpu.VMEM((width, height, NZ), jnp.int32),
            pltpu.VMEM((3, width, height, NZ), f32),
            pltpu.VMEM(send.shape, f32),
            pltpu.VMEM(forward.shape, f32),
            pltpu.VMEM(inverse.shape, f32),
            pltpu.VMEM((STEPS, 2, 5, height, NZ), f32),
            pltpu.VMEM((STEPS + 1, 2, 5, height, NZ), f32),
            pltpu.VMEM((STEPS, 2, 5 * width, 1, NZ), f32),
            pltpu.VMEM((STEPS + 1, 2, 5 * width, 1, NZ), f32),
            pltpu.VMEM((STEPS, 2, 2, 1, NZ), f32),
            pltpu.VMEM((STEPS + 1, 2, 2, 1, NZ), f32),
            pltpu.VMEM((count, 2, NZ), f32),
            pltpu.VMEM((count, 2, NZ), f32),
            pltpu.SemaphoreType.DMA((3,)),
            pltpu.SemaphoreType.DMA((3,)),
            pltpu.SemaphoreType.DMA((STEPS, MESSAGES)),
            pltpu.SemaphoreType.DMA((STEPS, MESSAGES)),
            pltpu.SemaphoreType.DMA,
            pltpu.SemaphoreType.DMA,
        ],
        compiler_params=pltpu.CompilerParams(
            collective_id=0, has_side_effects=True, vmem_limit_bytes=60 * 1024 * 1024
        ),
        name="cycle",
    )(pops, label, drive, send, forward, inverse)


def solution(mesh):
    nx, ny = mesh.shape["gx"], mesh.shape["gy"]
    constants = tuple(jnp.asarray(table) for table in tables(nx, ny))
    in_specs = (P(None, "gx", "gy", None), P("gx", "gy", None), P(None, "gx", "gy", None))
    out_specs = (P(None, "gx", "gy", None), P(None, "gx", "gy", None))
    return jax.shard_map(
        functools.partial(local, nx, ny, constants),
        mesh=mesh, in_specs=in_specs, out_specs=out_specs, check_vma=False,
    )
```

```python
import functools
import math

import jax
import jax.numpy as jnp
import numpy as np
from jax import lax
from jax.experimental import pallas as pl
from jax.experimental.pallas import tpu as pltpu
from jax.sharding import PartitionSpec as P

MESH = pl.DeviceIdType.MESH
NZ = 128
STEPS = 4
CUT = 4
VELOCITY = [
    (0, 0, 0),
    (1, 0, 0),
    (-1, 0, 0),
    (0, 1, 0),
    (0, -1, 0),
    (0, 0, 1),
    (0, 0, -1),
    (1, 1, 0),
    (-1, -1, 0),
    (1, -1, 0),
    (-1, 1, 0),
    (1, 0, 1),
    (-1, 0, -1),
    (1, 0, -1),
    (-1, 0, 1),
    (0, 1, 1),
    (0, -1, -1),
    (0, 1, -1),
    (0, -1, 1),
]
WEIGHTS = [1.0 / 3.0] + [1.0 / 18.0] * 6 + [1.0 / 36.0] * 12
SLOW_VISCOSITY = 0.0004
PAIRS = [(0, 0), (1, 1), (2, 2), (0, 1), (0, 2), (1, 2)]
EVEN = 4
CROSS = {
    (axis, sign): [i for i in range(19) if VELOCITY[i][axis] == sign] for axis in (0, 1) for sign in (1, -1)
}
MESSAGES = 8


def wave_table(length):
    index = np.arange(length)
    return 2.0 * np.pi * np.where(index >= (length + 1) // 2, index - length, index) / length


def response(nx, ny, nz):
    waves = np.meshgrid(wave_table(nx), wave_table(ny), wave_table(nz), indexing="ij")
    square = waves[0] ** 2 + waves[1] ** 2 + waves[2] ** 2
    safe = np.where(square > 0, square, 1.0)
    out = np.zeros((3, 6, nx, ny, nz // 2 + 1), np.complex128)
    for c, (p, q) in enumerate(PAIRS):
        force = [np.zeros_like(square) for _ in range(3)]
        force[p] = force[p] + waves[q]
        if p != q:
            force[q] = force[q] + waves[p]
        inner = sum(waves[a] * force[a] for a in range(3))
        for a in range(3):
            gain = np.where(square > 0, (force[a] - waves[a] * inner / safe) / (SLOW_VISCOSITY * safe), 0.0)
            mirror = np.roll(gain[::-1, ::-1, ::-1], (1, 1, 1), (0, 1, 2))
            odd = 0.5 * (gain - mirror)
            out[a, c] = np.fft.ifft2(-1j * odd, axes=(0, 1))[:, :, : nz // 2 + 1]
    return out


def split(table):
    table = table.astype(np.float32)
    high = table.astype(jnp.bfloat16)
    low = (table - high.astype(np.float32)).astype(jnp.bfloat16)
    return np.concatenate([high, low], axis=1)


def tables(nx, ny):
    slow = NZ // CUT
    half = slow // 2
    green = response(nx, 2 * ny, slow)
    count = nx * ny
    send = np.zeros((count, 12, 2, 4, slow))
    place = {(0, 0): (0, 0), (0, 1): (0, 1), (2, 0): (0, 2), (2, 1): (0, 3), (1, 0): (1, 0), (1, 1): (1, 1)}
    far_x = np.arange(count) // ny
    far_y = np.arange(count) % ny
    for c in range(6):
        for half_y in range(2):
            for (a, to_y), (row, block) in place.items():
                g = green[a, c][far_x, (2 * far_y + to_y - half_y) % (2 * ny)]
                inside = g[:, 1:half]
                if a < 2:
                    inside = inside.real if c < EVEN else inside.imag
                else:
                    inside = inside.imag if c < EVEN else -inside.real
                send[:, 2 * c + half_y, row, block, : half + 1] = g.real
                send[:, 2 * c + half_y, row, block, 1:half] = inside
                send[:, 2 * c + half_y, row, block, half + 1 :] = inside
    send = send.reshape(count // 4, 4, 12, 2, NZ).transpose(0, 2, 1, 3, 4).reshape(count // 4, 12, 8, NZ)
    place_z = np.arange(slow)
    angle = 2.0 * np.pi * place_z[:, None] * np.arange(half + 1)[None, :] / slow
    cosine, sine = np.cos(angle), np.sin(angle)
    plain = np.concatenate([cosine, -sine[:, 1:half]], axis=1)
    turned = np.concatenate([cosine[:, :1], sine[:, 1:half], cosine[:, half:], cosine[:, 1:half]], axis=1)
    scale = 1.0 / (STEPS * CUT**3)
    forward = np.stack([split(np.repeat(np.tile(one, (1, 4)), CUT, axis=0) * scale) for one in (plain, turned)])
    edge = [cosine[:, :1], cosine[:, half:]]
    back = np.concatenate([edge[0], 2 * cosine[:, 1:half], edge[1], -2 * sine[:, 1:half]], axis=1).T / slow
    back_turned = np.concatenate([edge[0], -2 * sine[:, 1:half], edge[1], -2 * cosine[:, 1:half]], axis=1).T / slow
    inverse = np.concatenate([back, back, back_turned, back_turned], axis=0)
    inverse = split(np.concatenate([inverse, np.zeros((NZ, NZ - slow))], axis=1))
    return send.astype(np.float32), forward, inverse


def dot(left, right):
    rows = left.shape[0]
    high = left.astype(jnp.bfloat16).astype(jnp.float32)
    parts = jnp.concatenate([high, left - high], axis=0).astype(jnp.bfloat16)
    both = jnp.dot(parts, right, preferred_element_type=jnp.float32)
    return both[:rows, :NZ] + (both[:rows, NZ:] + both[rows:, :NZ])


def moments(f):
    rho = f[0]
    for i in range(1, 19):
        rho = rho + f[i]
    j = []
    for axis in range(3):
        plus = [f[i] for i in range(19) if VELOCITY[i][axis] == 1]
        minus = [f[i] for i in range(19) if VELOCITY[i][axis] == -1]
        total = plus[0] - minus[0]
        for one, other in zip(plus[1:], minus[1:]):
            total = total + (one - other)
        j.append(total)
    return rho, j


def collide(f, rho, j, inverse, keep, omega, push, solid):
    speed = [one * inverse for one in j]
    square = speed[0] * speed[0] + speed[1] * speed[1] + speed[2] * speed[2]
    weight = omega * rho
    base = weight * (1.0 - 1.5 * square)
    quad = 4.5 * weight
    lead = [3.0 * (omega * j[a] + push[a]) for a in range(3)]
    post = [None] * 19
    post[0] = jnp.where(solid, f[0], keep * f[0] + WEIGHTS[0] * base)
    for i in range(1, 19, 2):
        along = linear = None
        for axis in range(3):
            c = VELOCITY[i][axis]
            if c:
                along = c * speed[axis] if along is None else along + speed[axis] if c > 0 else along - speed[axis]
                linear = c * lead[axis] if linear is None else linear + lead[axis] if c > 0 else linear - lead[axis]
        even = WEIGHTS[i] * (base + quad * (along * along))
        odd = WEIGHTS[i] * linear
        post[i] = jnp.where(solid, f[i + 1], keep * f[i] + (even + odd))
        post[i + 1] = jnp.where(solid, f[i], keep * f[i + 1] + (even - odd))
    return post


def kernel(
    nx, ny, pops_hbm, label_hbm, drive_hbm, table_hbm, forward_hbm, inverse_hbm, momentum, running_ref,
    state, stress, label, drive, table, forward, inverse_z, face_out, face_in, row_out, row_in, edge_out, edge_in,
    message, arrived, load_sem, const_sem, halo_send, halo_recv, slow_send, slow_recv,
):
    width = label.shape[0]
    gx = lax.axis_index("gx")
    gy = lax.axis_index("gy")
    count = nx * ny

    loads = [
        pltpu.make_async_copy(pops_hbm, state.at[0], load_sem.at[0]),
        pltpu.make_async_copy(label_hbm, label, load_sem.at[1]),
        pltpu.make_async_copy(drive_hbm, drive, load_sem.at[2]),
    ]
    constants = [
        pltpu.make_async_copy(table_hbm, table, const_sem.at[0]),
        pltpu.make_async_copy(forward_hbm, forward, const_sem.at[1]),
        pltpu.make_async_copy(inverse_hbm, inverse_z, const_sem.at[2]),
    ]
    def wrap(at, size):
        return jnp.where(at >= size, at - size, at)

    def over_others(body):
        for dy in range(1, ny):
            body(dy, (gx, wrap(gy + dy, ny)))

        def step(dx, carry):
            x = wrap(gx + dx, nx)
            for dy in range(ny):
                body(dx * ny + dy, (x, wrap(gy + dy, ny)))
            return carry

        lax.fori_loop(1, nx, step, 0)

    barrier = pltpu.get_barrier_semaphore()
    over_others(lambda far, place: pl.semaphore_signal(barrier, inc=1, device_id=place, device_id_type=MESH))
    for copy in loads + constants:
        copy.start()
    for c in range(6):
        stress[c] = jnp.zeros((8, NZ), jnp.float32)

    for copy in loads:
        copy.wait()

    east, west = wrap(gx + 1, nx), wrap(gx + nx - 1, nx)
    north, south = wrap(gy + 1, ny), wrap(gy + ny - 1, ny)
    side_x = {1: east, -1: west}
    side_y = {1: north, -1: south}
    slot = {1: 0, -1: 1}

    def remote(src, dst, step, number, place):
        return pltpu.make_async_remote_copy(
            src_ref=src,
            dst_ref=dst,
            send_sem=halo_send.at[step, number],
            recv_sem=halo_recv.at[step, number],
            device_id=place,
            device_id_type=MESH,
        )

    def halo(step):
        faces, rows = {}, []
        for sign in (1, -1):
            s = slot[sign]
            faces[sign] = [remote(face_out.at[step, s], face_in.at[step + 1, s], step, s, (side_x[sign], gy))]
            if ny == 2:
                faces[sign].append(
                    remote(edge_out.at[step, s], edge_in.at[step + 1, s], step, 4 + s, (side_x[sign], north))
                )
                continue
            for turn in (1, -1):
                t = slot[turn]
                faces[sign].append(
                    remote(
                        edge_out.at[step, s, t], edge_in.at[step + 1, s, t], step, 4 + 2 * s + t,
                        (side_x[sign], side_y[turn]),
                    )
                )
            rows.append(remote(row_out.at[step, s], row_in.at[step + 1, s], step, 2 + s, (gx, side_y[sign])))
        if ny == 2:
            rows.append(remote(row_out.at[step], row_in.at[step + 1], step, 2, (gx, north)))
        return faces, rows

    row_id = lax.broadcasted_iota(jnp.int32, (8, NZ), 0)

    def read(step, fresh, i, p):
        cx, cy, _ = VELOCITY[i]
        outside = (cx == 1 and p == 0) or (cx == -1 and p == width - 1)
        if outside:
            value = face_in[step, slot[cx], CROSS[0, cx].index(i)]
        else:
            value = state[step, i, p]
        if cy:
            if outside:
                row = edge_in[step, slot[cx], slot[cy]]
            else:
                row = row_in[step, slot[cy], CROSS[1, cy].index(i) * width + p]
            value = jnp.where(row_id == fresh[cy], jnp.broadcast_to(row, (8, NZ)), value)
        return value

    def write(step, i, p, value):
        cx, cy, cz = VELOCITY[i]
        if cz:
            value = pltpu.roll(value, cz % NZ, 1)
        if cy:
            value = pltpu.roll(value, cy % 8, 0)
            line = value[0:1] if cy == 1 else value[7:8]
        outside = (cx == 1 and p == width - 1) or (cx == -1 and p == 0)
        if outside:
            face_out[step, slot[cx], CROSS[0, cx].index(i)] = value
            if cy:
                edge_out[step, slot[cx], slot[cy]] = line
        else:
            state[step + 1, i, p + cx] = value
            if cy:
                row_out[step, slot[cy], CROSS[1, cy].index(i) * width + p + cx] = line

    def send_copy(far, place):
        return pltpu.make_async_remote_copy(
            src_ref=message.at[far],
            dst_ref=arrived.at[far],
            send_sem=slow_send,
            recv_sem=slow_recv,
            device_id=place,
            device_id_type=MESH,
        )

    def phase_of(step):
        quarter = math.cos(math.pi / 4.0)
        return jnp.where((step == 0) | (step == STEPS - 1), quarter, -quarter)

    def measure(step, planes):
        fresh = {1: jnp.where(step > 0, 0, -1), -1: jnp.where(step > 0, 7, -1)}
        total = [None] * 6
        held = []
        for p in planes:
            f = [read(step, fresh, i, p) for i in range(19)]
            rho, j = moments(f)
            inverse = 1.0 / rho
            thin = jnp.where(label[p] == 2, 0.0, inverse)
            scaled = [one * thin for one in j]
            for c, (a, b) in enumerate(PAIRS):
                term = scaled[a] * j[b]
                total[c] = term if total[c] is None else total[c] + term
            held.append((p, f, rho, j, inverse))
        for c in range(6):
            stress[c] += total[c]
        return held

    def finish(step, held):
        phase = phase_of(step)
        for p, f, rho, j, inverse in held:
            second = label[p] == 1
            omega = jnp.where(second, 1.1, 1.6)
            strength = jnp.where(second, 0.6 * phase, phase)
            push = [strength * drive[a, p] for a in range(3)]
            post = collide(f, rho, j, inverse, 1.0 - omega, omega, push, label[p] == 2)
            for i in range(19):
                write(step, i, p, post[i])

    def advance(step, planes):
        for p in planes:
            finish(step, measure(step, [p]))

    for sign in (1, -1):
        for k, i in enumerate(CROSS[0, sign]):
            face_in[0, slot[sign], k] = state[0, i, 0 if sign == 1 else width - 1]

    inner = list(range(1, width - 1))
    far_side = gx == nx - 1

    def start_step(step):
        for copy in halo(step - 1)[1]:
            copy.wait_recv()
        advance(step, inner)

    def side(step, sign):
        for copy in halo(step - 1)[0][-sign]:
            copy.wait_recv()
        advance(step, [width - 1 if sign == 1 else 0])
        for copy in halo(step)[0][sign]:
            copy.start()

    advance(0, [0, width - 1])
    pl.semaphore_wait(barrier, count - 1)
    faces, rows = halo(0)
    for copy in faces[1] + faces[-1]:
        copy.start()
    advance(0, inner)
    for copy in rows:
        copy.start()

    def cycle_step(step, carry):
        start_step(step)

        @pl.when(far_side)
        def _():
            side(step, -1)
            side(step, 1)

        @pl.when(jnp.logical_not(far_side))
        def _():
            side(step, 1)
            side(step, -1)

        for copy in halo(step)[1]:
            copy.start()
        return carry

    lax.fori_loop(1, STEPS - 1, cycle_step, 0)
    step = STEPS - 1
    start_step(step)
    for copy in constants:
        copy.wait()
    for sign in (1, -1):
        for copy in halo(step - 1)[0][sign]:
            copy.wait_recv()
    held = measure(step, [0, width - 1])
    plain = dot(stress[:EVEN].reshape(8 * EVEN, NZ), forward[0])
    turned = dot(stress[EVEN:].reshape(8 * (6 - EVEN), NZ), forward[1])
    finish(step, held)
    faces, rows = halo(step)
    last = faces[1] + faces[-1] + rows
    for copy in last:
        copy.start()

    lines = []
    for c in range(6):
        tile = plain[8 * c : 8 * c + 8] if c < EVEN else turned[8 * (c - EVEN) : 8 * (c - EVEN) + 8]
        tile = tile + pltpu.roll(tile, 7, 0)
        tile = tile + pltpu.roll(tile, 6, 0)
        lines.append(jnp.broadcast_to(tile[0:1], (8, NZ)))
        lines.append(jnp.broadcast_to(tile[4:5], (8, NZ)))

    def group(g):
        value = lines[0] * table[g, 0]
        for k in range(1, 12):
            value = value + lines[k] * table[g, k]
        for k in range(4):
            message[4 * g + k] = value[2 * k : 2 * k + 2]

    if count <= 64:
        for g in range(count // 4):
            group(g)
    else:
        def each(g, carry):
            group(g)
            return carry

        lax.fori_loop(0, count // 4, each, 0)
    over_others(lambda far, place: send_copy(far, place).start())

    for copy in last:
        copy.wait_recv()
    for p in range(width):
        f = [None] + [read(STEPS, {1: 0, -1: 7}, i, p) for i in range(1, 19)]
        for axis in range(3):
            value = None
            for i in range(1, 19):
                c = VELOCITY[i][axis]
                if c:
                    value = c * f[i] if value is None else value + f[i] if c > 0 else value - f[i]
            momentum[axis, p] = value
    for step in range(STEPS):
        faces, rows = halo(step)
        for copy in faces[1] + faces[-1] + rows:
            copy.wait_send()

    rest = pl.ds(1, count - 1)
    pltpu.make_async_copy(message.at[rest], arrived.at[rest], slow_recv).wait()
    spectrum = message[0]
    if count <= 64:
        for far in range(1, count):
            spectrum = spectrum + arrived[far]
    else:
        spectrum = lax.fori_loop(1, count, lambda far, value: value + arrived[far], spectrum)
    upper = jnp.broadcast_to(spectrum[0:1], (8, NZ))
    lower = jnp.broadcast_to(spectrum[1:2], (8, NZ))
    lane = lax.broadcasted_iota(jnp.int32, (8, NZ), 1)
    slow_z = NZ // CUT
    block = row_id % 2 + jnp.where(row_id >= 4, 2, 0)
    low = slow_z * block
    spread = jnp.where((row_id == 2) | (row_id == 3), lower, upper)
    spread = jnp.where((lane >= low) & (lane < low + slow_z), spread, 0.0)
    result = dot(spread, inverse_z[...])
    for a in range(3):
        running_ref[a, 0] = result[2 * a : 2 * a + 2, :slow_z]
    pltpu.make_async_copy(arrived.at[rest], message.at[rest], slow_send).wait()


def local(nx, ny, constants, pops, label, drive):
    width, height = pops.shape[1], pops.shape[2]
    count = nx * ny
    send, forward, inverse = constants
    anywhere = pl.BlockSpec(memory_space=pltpu.HBM)
    f32 = jnp.float32
    return pl.pallas_call(
        functools.partial(kernel, nx, ny),
        out_shape=(
            pltpu.VMEM((3, width, height, NZ), f32),
            pltpu.VMEM((3, width // CUT, height // CUT, NZ // CUT), f32),
        ),
        in_specs=[anywhere] * 6,
        out_specs=(pl.BlockSpec(memory_space=pltpu.VMEM),) * 2,
        scratch_shapes=[
            pltpu.VMEM((STEPS + 1, 19, width, height, NZ), f32),
            pltpu.VMEM((6, height, NZ), f32),
            pltpu.VMEM((width, height, NZ), jnp.int32),
            pltpu.VMEM((3, width, height, NZ), f32),
            pltpu.VMEM(send.shape, f32),
            pltpu.VMEM(forward.shape, forward.dtype),
            pltpu.VMEM(inverse.shape, inverse.dtype),
            pltpu.VMEM((STEPS, 2, 5, height, NZ), f32),
            pltpu.VMEM((STEPS + 1, 2, 5, height, NZ), f32),
            pltpu.VMEM((STEPS, 2, 5 * width, 1, NZ), f32),
            pltpu.VMEM((STEPS + 1, 2, 5 * width, 1, NZ), f32),
            pltpu.VMEM((STEPS, 2, 2, 1, NZ), f32),
            pltpu.VMEM((STEPS + 1, 2, 2, 1, NZ), f32),
            pltpu.VMEM((count, 2, NZ), f32),
            pltpu.VMEM((count, 2, NZ), f32),
            pltpu.SemaphoreType.DMA((3,)),
            pltpu.SemaphoreType.DMA((3,)),
            pltpu.SemaphoreType.DMA((STEPS, MESSAGES)),
            pltpu.SemaphoreType.DMA((STEPS, MESSAGES)),
            pltpu.SemaphoreType.DMA,
            pltpu.SemaphoreType.DMA,
        ],
        compiler_params=pltpu.CompilerParams(
            collective_id=0, has_side_effects=True, vmem_limit_bytes=60 * 1024 * 1024
        ),
        name="cycle",
    )(pops, label, drive, send, forward, inverse)


def solution(mesh):
    nx, ny = mesh.shape["gx"], mesh.shape["gy"]
    constants = tuple(jnp.asarray(table) for table in tables(nx, ny))
    in_specs = (P(None, "gx", "gy", None), P("gx", "gy", None), P(None, "gx", "gy", None))
    out_specs = (P(None, "gx", "gy", None), P(None, "gx", "gy", None))
    return jax.shard_map(
        functools.partial(local, nx, ny, constants),
        mesh=mesh, in_specs=in_specs, out_specs=out_specs, check_vma=False,
    )
```

```python
import functools
import math

import jax
import jax.numpy as jnp
import numpy as np
from jax import lax
from jax.experimental import pallas as pl
from jax.experimental.pallas import tpu as pltpu
from jax.sharding import PartitionSpec as P

MESH = pl.DeviceIdType.MESH
NZ = 128
STEPS = 4
CUT = 4
VELOCITY = [
    (0, 0, 0),
    (1, 0, 0),
    (-1, 0, 0),
    (0, 1, 0),
    (0, -1, 0),
    (0, 0, 1),
    (0, 0, -1),
    (1, 1, 0),
    (-1, -1, 0),
    (1, -1, 0),
    (-1, 1, 0),
    (1, 0, 1),
    (-1, 0, -1),
    (1, 0, -1),
    (-1, 0, 1),
    (0, 1, 1),
    (0, -1, -1),
    (0, 1, -1),
    (0, -1, 1),
]
WEIGHTS = [1.0 / 3.0] + [1.0 / 18.0] * 6 + [1.0 / 36.0] * 12
SLOW_VISCOSITY = 0.0004
PAIRS = [(0, 0), (1, 1), (2, 2), (0, 1), (0, 2), (1, 2)]
EVEN = 4
CROSS = {
    (axis, sign): [i for i in range(19) if VELOCITY[i][axis] == sign] for axis in (0, 1) for sign in (1, -1)
}
GROUP = 4
MESSAGES = 8


def wave_table(length):
    index = np.arange(length)
    return 2.0 * np.pi * np.where(index >= (length + 1) // 2, index - length, index) / length


def response(nx, ny, nz):
    waves = np.meshgrid(wave_table(nx), wave_table(ny), wave_table(nz), indexing="ij")
    square = waves[0] ** 2 + waves[1] ** 2 + waves[2] ** 2
    safe = np.where(square > 0, square, 1.0)
    out = np.zeros((3, 6, nx, ny, nz // 2 + 1), np.complex128)
    for c, (p, q) in enumerate(PAIRS):
        force = [np.zeros_like(square) for _ in range(3)]
        force[p] = force[p] + waves[q]
        if p != q:
            force[q] = force[q] + waves[p]
        inner = sum(waves[a] * force[a] for a in range(3))
        for a in range(3):
            gain = np.where(square > 0, (force[a] - waves[a] * inner / safe) / (SLOW_VISCOSITY * safe), 0.0)
            mirror = np.roll(gain[::-1, ::-1, ::-1], (1, 1, 1), (0, 1, 2))
            odd = 0.5 * (gain - mirror)
            out[a, c] = np.fft.ifft2(-1j * odd, axes=(0, 1))[:, :, : nz // 2 + 1]
    return out


def split(table):
    table = table.astype(np.float32)
    high = table.astype(jnp.bfloat16)
    low = (table - high.astype(np.float32)).astype(jnp.bfloat16)
    return np.concatenate([high, low], axis=1)


def tables(nx, ny):
    slow = NZ // CUT
    half = slow // 2
    green = response(nx, 2 * ny, slow)
    count = nx * ny
    send = np.zeros((GROUP, count, 12, 2, 4, slow))
    place = {(0, 0): (0, 0), (0, 1): (0, 1), (2, 0): (0, 2), (2, 1): (0, 3), (1, 0): (1, 0), (1, 1): (1, 1)}
    far_x = np.arange(count) // ny - np.arange(GROUP)[:, None]
    far_y = np.arange(count) % ny + np.zeros((GROUP, 1), np.int64)
    for c in range(6):
        for half_y in range(2):
            for (a, to_y), (row, block) in place.items():
                g = green[a, c][far_x % nx, (2 * far_y + to_y - half_y) % (2 * ny)]
                inside = g[..., 1:half]
                if a < 2:
                    inside = inside.real if c < EVEN else inside.imag
                else:
                    inside = inside.imag if c < EVEN else -inside.real
                send[:, :, 2 * c + half_y, row, block, : half + 1] = g.real
                send[:, :, 2 * c + half_y, row, block, 1:half] = inside
                send[:, :, 2 * c + half_y, row, block, half + 1 :] = inside
    send = send.reshape(GROUP, count // 4, 4, 12, 2, NZ).transpose(0, 1, 3, 2, 4, 5).reshape(GROUP, count // 4, 12, 8, NZ)
    place_z = np.arange(slow)
    angle = 2.0 * np.pi * place_z[:, None] * np.arange(half + 1)[None, :] / slow
    cosine, sine = np.cos(angle), np.sin(angle)
    plain = np.concatenate([cosine, -sine[:, 1:half]], axis=1)
    turned = np.concatenate([cosine[:, :1], sine[:, 1:half], cosine[:, half:], cosine[:, 1:half]], axis=1)
    scale = 1.0 / (STEPS * CUT**3)
    forward = np.stack([split(np.repeat(np.tile(one, (1, 4)), CUT, axis=0) * scale) for one in (plain, turned)])
    edge = [cosine[:, :1], cosine[:, half:]]
    back = np.concatenate([edge[0], 2 * cosine[:, 1:half], edge[1], -2 * sine[:, 1:half]], axis=1).T / slow
    back_turned = np.concatenate([edge[0], -2 * sine[:, 1:half], edge[1], -2 * cosine[:, 1:half]], axis=1).T / slow
    inverse = np.concatenate([back, back, back_turned, back_turned], axis=0)
    inverse = split(np.concatenate([inverse, np.zeros((NZ, NZ - slow))], axis=1))
    return send.astype(np.float32), forward, inverse


def dot(left, right):
    rows = left.shape[0]
    high = left.astype(jnp.bfloat16).astype(jnp.float32)
    parts = jnp.concatenate([high, left - high], axis=0).astype(jnp.bfloat16)
    both = jnp.dot(parts, right, preferred_element_type=jnp.float32)
    return both[:rows, :NZ] + (both[:rows, NZ:] + both[rows:, :NZ])


def moments(f):
    rho = f[0]
    for i in range(1, 19):
        rho = rho + f[i]
    j = []
    for axis in range(3):
        plus = [f[i] for i in range(19) if VELOCITY[i][axis] == 1]
        minus = [f[i] for i in range(19) if VELOCITY[i][axis] == -1]
        total = plus[0] - minus[0]
        for one, other in zip(plus[1:], minus[1:]):
            total = total + (one - other)
        j.append(total)
    return rho, j


def collide(f, rho, j, inverse, keep, omega, push, solid):
    speed = [one * inverse for one in j]
    square = speed[0] * speed[0] + speed[1] * speed[1] + speed[2] * speed[2]
    weight = omega * rho
    base = weight * (1.0 - 1.5 * square)
    quad = 4.5 * weight
    lead = [3.0 * (omega * j[a] + push[a]) for a in range(3)]
    post = [None] * 19
    post[0] = jnp.where(solid, f[0], keep * f[0] + WEIGHTS[0] * base)
    for i in range(1, 19, 2):
        along = linear = None
        for axis in range(3):
            c = VELOCITY[i][axis]
            if c:
                along = c * speed[axis] if along is None else along + speed[axis] if c > 0 else along - speed[axis]
                linear = c * lead[axis] if linear is None else linear + lead[axis] if c > 0 else linear - lead[axis]
        even = WEIGHTS[i] * (base + quad * (along * along))
        odd = WEIGHTS[i] * linear
        post[i] = jnp.where(solid, f[i + 1], keep * f[i] + (even + odd))
        post[i + 1] = jnp.where(solid, f[i], keep * f[i + 1] + (even - odd))
    return post


def kernel(
    nx, ny, pops_hbm, label_hbm, drive_hbm, table_hbm, forward_hbm, inverse_hbm, momentum, running_ref,
    state, stress, label, drive, table, forward, inverse_z, face_out, face_in, row_out, row_in, edge_out, edge_in,
    message, arrived, summed, final, load_sem, const_sem, halo_send, halo_recv, slow_send, slow_recv,
):
    width = label.shape[0]
    gx = lax.axis_index("gx")
    gy = lax.axis_index("gy")
    count = nx * ny

    loads = [
        pltpu.make_async_copy(pops_hbm, state.at[0], load_sem.at[0]),
        pltpu.make_async_copy(label_hbm, label, load_sem.at[1]),
        pltpu.make_async_copy(drive_hbm, drive, load_sem.at[2]),
    ]
    constants = [
        pltpu.make_async_copy(table_hbm.at[lax.rem(gx, GROUP)], table, const_sem.at[0]),
        pltpu.make_async_copy(forward_hbm, forward, const_sem.at[1]),
        pltpu.make_async_copy(inverse_hbm, inverse_z, const_sem.at[2]),
    ]
    def wrap(at, size):
        return jnp.where(at >= size, at - size, at)

    east, west = wrap(gx + 1, nx), wrap(gx + nx - 1, nx)
    north, south = wrap(gy + 1, ny), wrap(gy + ny - 1, ny)
    side_x = {1: east, -1: west}
    side_y = {1: north, -1: south}
    groups = nx // GROUP
    share = GROUP * ny
    place = lax.rem(gx, GROUP)
    base = gx - place
    edges = [north] if ny == 2 else [north, south]
    friends = [(x, y) for x in (east, west) for y in [gy] + edges] + [(gx, y) for y in edges]
    afar = [(wrap(gx + GROUP * k, nx), gy) for k in range(1, groups)]
    near = []
    for k in range(1, share):
        at = wrap(place + k // ny, GROUP)
        near.append((at * ny + k % ny, (base + at, wrap(gy + k % ny, ny))))
    greeted = friends + afar + [spot for _, spot in near]
    barrier = pltpu.get_barrier_semaphore()
    for spot in greeted:
        pl.semaphore_signal(barrier, inc=1, device_id=spot, device_id_type=MESH)
    for copy in loads + constants:
        copy.start()
    for c in range(6):
        stress[c] = jnp.zeros((8, NZ), jnp.float32)

    for copy in loads:
        copy.wait()

    slot = {1: 0, -1: 1}

    def remote(src, dst, step, number, place):
        return pltpu.make_async_remote_copy(
            src_ref=src,
            dst_ref=dst,
            send_sem=halo_send.at[step, number],
            recv_sem=halo_recv.at[step, number],
            device_id=place,
            device_id_type=MESH,
        )

    def halo(step):
        faces, rows = {}, []
        for sign in (1, -1):
            s = slot[sign]
            faces[sign] = [remote(face_out.at[step, s], face_in.at[step + 1, s], step, s, (side_x[sign], gy))]
            if ny == 2:
                faces[sign].append(
                    remote(edge_out.at[step, s], edge_in.at[step + 1, s], step, 4 + s, (side_x[sign], north))
                )
                continue
            for turn in (1, -1):
                t = slot[turn]
                faces[sign].append(
                    remote(
                        edge_out.at[step, s, t], edge_in.at[step + 1, s, t], step, 4 + 2 * s + t,
                        (side_x[sign], side_y[turn]),
                    )
                )
            rows.append(remote(row_out.at[step, s], row_in.at[step + 1, s], step, 2 + s, (gx, side_y[sign])))
        if ny == 2:
            rows.append(remote(row_out.at[step], row_in.at[step + 1], step, 2, (gx, north)))
        return faces, rows

    row_id = lax.broadcasted_iota(jnp.int32, (8, NZ), 0)

    def read(step, fresh, i, p):
        cx, cy, _ = VELOCITY[i]
        outside = (cx == 1 and p == 0) or (cx == -1 and p == width - 1)
        if outside:
            value = face_in[step, slot[cx], CROSS[0, cx].index(i)]
        else:
            value = state[step, i, p]
        if cy:
            if outside:
                row = edge_in[step, slot[cx], slot[cy]]
            else:
                row = row_in[step, slot[cy], CROSS[1, cy].index(i) * width + p]
            value = jnp.where(row_id == fresh[cy], jnp.broadcast_to(row, (8, NZ)), value)
        return value

    def write(step, i, p, value):
        cx, cy, cz = VELOCITY[i]
        if cz:
            value = pltpu.roll(value, cz % NZ, 1)
        if cy:
            value = pltpu.roll(value, cy % 8, 0)
            line = value[0:1] if cy == 1 else value[7:8]
        outside = (cx == 1 and p == width - 1) or (cx == -1 and p == 0)
        if outside:
            face_out[step, slot[cx], CROSS[0, cx].index(i)] = value
            if cy:
                edge_out[step, slot[cx], slot[cy]] = line
        else:
            state[step + 1, i, p + cx] = value
            if cy:
                row_out[step, slot[cy], CROSS[1, cy].index(i) * width + p + cx] = line

    def slow_copy(src, dst, stage, spot):
        return pltpu.make_async_remote_copy(
            src_ref=src,
            dst_ref=dst,
            send_sem=slow_send.at[stage],
            recv_sem=slow_recv.at[stage],
            device_id=spot,
            device_id_type=MESH,
        )

    def phase_of(step):
        quarter = math.cos(math.pi / 4.0)
        return jnp.where((step == 0) | (step == STEPS - 1), quarter, -quarter)

    def measure(step, planes):
        fresh = {1: jnp.where(step > 0, 0, -1), -1: jnp.where(step > 0, 7, -1)}
        total = [None] * 6
        held = []
        for p in planes:
            f = [read(step, fresh, i, p) for i in range(19)]
            rho, j = moments(f)
            inverse = 1.0 / rho
            thin = jnp.where(label[p] == 2, 0.0, inverse)
            scaled = [one * thin for one in j]
            for c, (a, b) in enumerate(PAIRS):
                term = scaled[a] * j[b]
                total[c] = term if total[c] is None else total[c] + term
            held.append((p, f, rho, j, inverse))
        for c in range(6):
            stress[c] += total[c]
        return held

    def finish(step, held):
        phase = phase_of(step)
        for p, f, rho, j, inverse in held:
            second = label[p] == 1
            omega = jnp.where(second, 1.1, 1.6)
            strength = jnp.where(second, 0.6 * phase, phase)
            push = [strength * drive[a, p] for a in range(3)]
            post = collide(f, rho, j, inverse, 1.0 - omega, omega, push, label[p] == 2)
            for i in range(19):
                write(step, i, p, post[i])

    def advance(step, planes):
        for p in planes:
            finish(step, measure(step, [p]))

    for sign in (1, -1):
        for k, i in enumerate(CROSS[0, sign]):
            face_in[0, slot[sign], k] = state[0, i, 0 if sign == 1 else width - 1]

    inner = list(range(1, width - 1))
    far_side = gx == nx - 1

    def start_step(step):
        for copy in halo(step - 1)[1]:
            copy.wait_recv()
        advance(step, inner)

    def side(step, sign):
        for copy in halo(step - 1)[0][-sign]:
            copy.wait_recv()
        advance(step, [width - 1 if sign == 1 else 0])
        for copy in halo(step)[0][sign]:
            copy.start()

    advance(0, [0, width - 1])
    pl.semaphore_wait(barrier, len(greeted))
    faces, rows = halo(0)
    for copy in faces[1] + faces[-1]:
        copy.start()
    advance(0, inner)
    for copy in rows:
        copy.start()

    def cycle_step(step, carry):
        start_step(step)

        @pl.when(far_side)
        def _():
            side(step, -1)
            side(step, 1)

        @pl.when(jnp.logical_not(far_side))
        def _():
            side(step, 1)
            side(step, -1)

        for copy in halo(step)[1]:
            copy.start()
        return carry

    lax.fori_loop(1, STEPS - 1, cycle_step, 0)
    step = STEPS - 1
    start_step(step)
    for copy in constants:
        copy.wait()
    for sign in (1, -1):
        for copy in halo(step - 1)[0][sign]:
            copy.wait_recv()
    held = measure(step, [0, width - 1])
    plain = dot(stress[:EVEN].reshape(8 * EVEN, NZ), forward[0])
    turned = dot(stress[EVEN:].reshape(8 * (6 - EVEN), NZ), forward[1])
    finish(step, held)
    faces, rows = halo(step)
    last = faces[1] + faces[-1] + rows
    for copy in last:
        copy.start()

    lines = []
    for c in range(6):
        tile = plain[8 * c : 8 * c + 8] if c < EVEN else turned[8 * (c - EVEN) : 8 * (c - EVEN) + 8]
        tile = tile + pltpu.roll(tile, 7, 0)
        tile = tile + pltpu.roll(tile, 6, 0)
        lines.append(jnp.broadcast_to(tile[0:1], (8, NZ)))
        lines.append(jnp.broadcast_to(tile[4:5], (8, NZ)))

    def shares(k):
        for g in range(share // 4):
            row = k * (share // 4) + g
            value = lines[0] * table[row, 0]
            for n in range(1, 12):
                value = value + lines[n] * table[row, n]
            for n in range(4):
                message[k, 4 * g + n] = value[2 * n : 2 * n + 2]

    if count <= 64:
        for k in range(groups):
            shares(k)
    else:
        def each(k, carry):
            shares(k)
            return carry

        lax.fori_loop(0, groups, each, 0)
    for k in range(1, groups):
        slow_copy(message.at[k], arrived.at[k], 0, afar[k - 1]).start()
    others = pl.ds(1, groups - 1)
    pltpu.make_async_copy(message.at[others], arrived.at[others], slow_recv.at[0]).wait()
    value = message[0]
    for k in range(1, groups):
        value = value + arrived[k]
    summed[...] = value
    for k in range(1, share):
        target, spot = near[k - 1]
        slow_copy(summed.at[target], final.at[k], 1, spot).start()

    for copy in last:
        copy.wait_recv()
    for p in range(width):
        f = [None] + [read(STEPS, {1: 0, -1: 7}, i, p) for i in range(1, 19)]
        for axis in range(3):
            value = None
            for i in range(1, 19):
                c = VELOCITY[i][axis]
                if c:
                    value = c * f[i] if value is None else value + f[i] if c > 0 else value - f[i]
            momentum[axis, p] = value
    for step in range(STEPS):
        faces, rows = halo(step)
        for copy in faces[1] + faces[-1] + rows:
            copy.wait_send()

    rest = pl.ds(1, share - 1)
    pltpu.make_async_copy(summed.at[rest], final.at[rest], slow_recv.at[1]).wait()
    spectrum = summed[place * ny]
    for k in range(1, share):
        spectrum = spectrum + final[k]
    upper = jnp.broadcast_to(spectrum[0:1], (8, NZ))
    lower = jnp.broadcast_to(spectrum[1:2], (8, NZ))
    lane = lax.broadcasted_iota(jnp.int32, (8, NZ), 1)
    slow_z = NZ // CUT
    block = row_id % 2 + jnp.where(row_id >= 4, 2, 0)
    low = slow_z * block
    spread = jnp.where((row_id == 2) | (row_id == 3), lower, upper)
    spread = jnp.where((lane >= low) & (lane < low + slow_z), spread, 0.0)
    result = dot(spread, inverse_z[...])
    for a in range(3):
        running_ref[a, 0] = result[2 * a : 2 * a + 2, :slow_z]
    pltpu.make_async_copy(arrived.at[others], message.at[others], slow_send.at[0]).wait()
    pltpu.make_async_copy(final.at[rest], summed.at[rest], slow_send.at[1]).wait()


def local(nx, ny, constants, pops, label, drive):
    width, height = pops.shape[1], pops.shape[2]
    send, forward, inverse = constants
    anywhere = pl.BlockSpec(memory_space=pltpu.HBM)
    f32 = jnp.float32
    return pl.pallas_call(
        functools.partial(kernel, nx, ny),
        out_shape=(
            pltpu.VMEM((3, width, height, NZ), f32),
            pltpu.VMEM((3, width // CUT, height // CUT, NZ // CUT), f32),
        ),
        in_specs=[anywhere] * 6,
        out_specs=(pl.BlockSpec(memory_space=pltpu.VMEM),) * 2,
        scratch_shapes=[
            pltpu.VMEM((STEPS + 1, 19, width, height, NZ), f32),
            pltpu.VMEM((6, height, NZ), f32),
            pltpu.VMEM((width, height, NZ), jnp.int32),
            pltpu.VMEM((3, width, height, NZ), f32),
            pltpu.VMEM(send.shape[1:], f32),
            pltpu.VMEM(forward.shape, forward.dtype),
            pltpu.VMEM(inverse.shape, inverse.dtype),
            pltpu.VMEM((STEPS, 2, 5, height, NZ), f32),
            pltpu.VMEM((STEPS + 1, 2, 5, height, NZ), f32),
            pltpu.VMEM((STEPS, 2, 5 * width, 1, NZ), f32),
            pltpu.VMEM((STEPS + 1, 2, 5 * width, 1, NZ), f32),
            pltpu.VMEM((STEPS, 2, 2, 1, NZ), f32),
            pltpu.VMEM((STEPS + 1, 2, 2, 1, NZ), f32),
            pltpu.VMEM((nx // GROUP, GROUP * ny, 2, NZ), f32),
            pltpu.VMEM((nx // GROUP, GROUP * ny, 2, NZ), f32),
            pltpu.VMEM((GROUP * ny, 2, NZ), f32),
            pltpu.VMEM((GROUP * ny, 2, NZ), f32),
            pltpu.SemaphoreType.DMA((3,)),
            pltpu.SemaphoreType.DMA((3,)),
            pltpu.SemaphoreType.DMA((STEPS, MESSAGES)),
            pltpu.SemaphoreType.DMA((STEPS, MESSAGES)),
            pltpu.SemaphoreType.DMA((2,)),
            pltpu.SemaphoreType.DMA((2,)),
        ],
        compiler_params=pltpu.CompilerParams(
            collective_id=0, has_side_effects=True, vmem_limit_bytes=60 * 1024 * 1024
        ),
        name="cycle",
    )(pops, label, drive, send, forward, inverse)


def solution(mesh):
    nx, ny = mesh.shape["gx"], mesh.shape["gy"]
    constants = tuple(jnp.asarray(table) for table in tables(nx, ny))
    in_specs = (P(None, "gx", "gy", None), P("gx", "gy", None), P(None, "gx", "gy", None))
    out_specs = (P(None, "gx", "gy", None), P(None, "gx", "gy", None))
    return jax.shard_map(
        functools.partial(local, nx, ny, constants),
        mesh=mesh, in_specs=in_specs, out_specs=out_specs, check_vma=False,
    )
```

```python
import functools
import math

import jax
import jax.numpy as jnp
import numpy as np
from jax import lax
from jax.experimental import pallas as pl
from jax.experimental.pallas import tpu as pltpu
from jax.sharding import PartitionSpec as P

MESH = pl.DeviceIdType.MESH
NZ = 128
STEPS = 4
CUT = 4
VELOCITY = [
    (0, 0, 0),
    (1, 0, 0),
    (-1, 0, 0),
    (0, 1, 0),
    (0, -1, 0),
    (0, 0, 1),
    (0, 0, -1),
    (1, 1, 0),
    (-1, -1, 0),
    (1, -1, 0),
    (-1, 1, 0),
    (1, 0, 1),
    (-1, 0, -1),
    (1, 0, -1),
    (-1, 0, 1),
    (0, 1, 1),
    (0, -1, -1),
    (0, 1, -1),
    (0, -1, 1),
]
WEIGHTS = [1.0 / 3.0] + [1.0 / 18.0] * 6 + [1.0 / 36.0] * 12
SLOW_VISCOSITY = 0.0004
PAIRS = [(0, 0), (1, 1), (2, 2), (0, 1), (0, 2), (1, 2)]
EVEN = 4
ORDER = [i for sign in (1, 0, -1) for i in range(19) if VELOCITY[i][0] == sign]
KEPT = {i: n for n, i in enumerate(ORDER)}
UP, STAY = 5, 14
CROSS = {(axis, sign): [i for i in ORDER if VELOCITY[i][axis] == sign] for axis in (0, 1) for sign in (1, -1)}
PAD = 2
MESSAGES = 8
WIDE = 32


def wave_table(length):
    index = np.arange(length)
    return 2.0 * np.pi * np.where(index >= (length + 1) // 2, index - length, index) / length


def response(nx, ny, nz):
    waves = np.meshgrid(wave_table(nx), wave_table(ny), wave_table(nz), indexing="ij")
    square = waves[0] ** 2 + waves[1] ** 2 + waves[2] ** 2
    safe = np.where(square > 0, square, 1.0)
    out = np.zeros((3, 6, nx, ny, nz // 2 + 1), np.complex128)
    for c, (p, q) in enumerate(PAIRS):
        force = [np.zeros_like(square) for _ in range(3)]
        force[p] = force[p] + waves[q]
        if p != q:
            force[q] = force[q] + waves[p]
        inner = sum(waves[a] * force[a] for a in range(3))
        for a in range(3):
            gain = np.where(square > 0, (force[a] - waves[a] * inner / safe) / (SLOW_VISCOSITY * safe), 0.0)
            mirror = np.roll(gain[::-1, ::-1, ::-1], (1, 1, 1), (0, 1, 2))
            odd = 0.5 * (gain - mirror)
            out[a, c] = np.fft.ifft2(-1j * odd, axes=(0, 1))[:, :, : nz // 2 + 1]
    return out


def split(table):
    table = table.astype(np.float32)
    high = table.astype(jnp.bfloat16)
    low = (table - high.astype(np.float32)).astype(jnp.bfloat16)
    return np.concatenate([high, low], axis=1)


def tables(nx, ny):
    slow = NZ // CUT
    half = slow // 2
    green = response(nx, 2 * ny, slow)
    count = nx * ny
    send = np.zeros((count, 12, 2, 4, slow))
    place = {(0, 0): (0, 0), (0, 1): (0, 1), (2, 0): (0, 2), (2, 1): (0, 3), (1, 0): (1, 0), (1, 1): (1, 1)}
    far_x = np.arange(count) // ny
    far_y = np.arange(count) % ny
    for c in range(6):
        for half_y in range(2):
            for (a, to_y), (row, block) in place.items():
                g = green[a, c][far_x, (2 * far_y + to_y - half_y) % (2 * ny)]
                inside = g[:, 1:half]
                if a < 2:
                    inside = inside.real if c < EVEN else inside.imag
                else:
                    inside = inside.imag if c < EVEN else -inside.real
                send[:, 2 * c + half_y, row, block, : half + 1] = g.real
                send[:, 2 * c + half_y, row, block, 1:half] = inside
                send[:, 2 * c + half_y, row, block, half + 1 :] = inside
    send = send.reshape(count // 4, 4, 12, 2, NZ).transpose(0, 2, 1, 3, 4).reshape(count // 4, 12, 8, NZ)
    place_z = np.arange(slow)
    angle = 2.0 * np.pi * place_z[:, None] * np.arange(half + 1)[None, :] / slow
    cosine, sine = np.cos(angle), np.sin(angle)
    plain = np.concatenate([cosine, -sine[:, 1:half]], axis=1)
    turned = np.concatenate([cosine[:, :1], sine[:, 1:half], cosine[:, half:], cosine[:, 1:half]], axis=1)
    scale = 1.0 / (STEPS * CUT**3)
    forward = np.stack([split(np.repeat(np.tile(one, (1, 4)), CUT, axis=0) * scale) for one in (plain, turned)])
    edge = [cosine[:, :1], cosine[:, half:]]
    back = np.concatenate([edge[0], 2 * cosine[:, 1:half], edge[1], -2 * sine[:, 1:half]], axis=1).T / slow
    back_turned = np.concatenate([edge[0], -2 * sine[:, 1:half], edge[1], -2 * cosine[:, 1:half]], axis=1).T / slow
    inverse = np.concatenate([back, back, back_turned, back_turned], axis=0)
    inverse = split(np.concatenate([inverse, np.zeros((NZ, NZ - slow))], axis=1))
    return send.astype(np.float32), forward, inverse


def dot(left, right):
    rows = left.shape[0]
    high = left.astype(jnp.bfloat16).astype(jnp.float32)
    parts = jnp.concatenate([high, left - high], axis=0).astype(jnp.bfloat16)
    both = jnp.dot(parts, right, preferred_element_type=jnp.float32)
    return both[:rows, :NZ] + (both[:rows, NZ:] + both[rows:, :NZ])


def moments(f):
    rho = f[0]
    for i in range(1, 19):
        rho = rho + f[i]
    j = []
    for axis in range(3):
        plus = [f[i] for i in range(19) if VELOCITY[i][axis] == 1]
        minus = [f[i] for i in range(19) if VELOCITY[i][axis] == -1]
        total = plus[0] - minus[0]
        for one, other in zip(plus[1:], minus[1:]):
            total = total + (one - other)
        j.append(total)
    return rho, j


def collide(f, rho, j, inverse, keep, omega, push, solid):
    speed = [one * inverse for one in j]
    square = speed[0] * speed[0] + speed[1] * speed[1] + speed[2] * speed[2]
    weight = omega * rho
    base = weight * (1.0 - 1.5 * square)
    quad = 4.5 * weight
    lead = [3.0 * (omega * j[a] + push[a]) for a in range(3)]
    post = [None] * 19
    post[0] = jnp.where(solid, f[0], keep * f[0] + WEIGHTS[0] * base)
    for i in range(1, 19, 2):
        along = linear = None
        for axis in range(3):
            c = VELOCITY[i][axis]
            if c:
                along = c * speed[axis] if along is None else along + speed[axis] if c > 0 else along - speed[axis]
                linear = c * lead[axis] if linear is None else linear + lead[axis] if c > 0 else linear - lead[axis]
        even = WEIGHTS[i] * (base + quad * (along * along))
        odd = WEIGHTS[i] * linear
        post[i] = jnp.where(solid, f[i + 1], keep * f[i] + (even + odd))
        post[i + 1] = jnp.where(solid, f[i], keep * f[i + 1] + (even - odd))
    return post


def kernel(
    nx, ny, pops_hbm, label_hbm, drive_hbm, table_hbm, forward_hbm, inverse_hbm, momentum, running_ref,
    raw, state, stress, label, drive, table, forward, inverse_z, face_out, face_in, row_out, row_in, edge_out, edge_in,
    message, arrived, load_sem, const_sem, wide_send, wide_recv, halo_send, halo_recv, slow_send, slow_recv,
):
    width = raw.shape[1]
    own = pl.ds(PAD, width)
    gx = lax.axis_index("gx")
    gy = lax.axis_index("gy")
    count = nx * ny

    loads = [
        pltpu.make_async_copy(pops_hbm, raw, load_sem.at[0]),
        pltpu.make_async_copy(label_hbm, label.at[own], load_sem.at[1]),
        pltpu.make_async_copy(drive_hbm, drive.at[:, own], load_sem.at[2]),
    ]
    constants = [
        pltpu.make_async_copy(table_hbm, table, const_sem.at[0]),
        pltpu.make_async_copy(forward_hbm, forward, const_sem.at[1]),
        pltpu.make_async_copy(inverse_hbm, inverse_z, const_sem.at[2]),
    ]
    def wrap(at, size):
        return jnp.where(at >= size, at - size, at)

    def over_others(body):
        for dy in range(1, ny):
            body(dy, (gx, wrap(gy + dy, ny)))

        def step(dx, carry):
            x = wrap(gx + dx, nx)
            for dy in range(ny):
                body(dx * ny + dy, (x, wrap(gy + dy, ny)))
            return carry

        lax.fori_loop(1, nx, step, 0)

    barrier = pltpu.get_barrier_semaphore()
    over_others(lambda far, place: pl.semaphore_signal(barrier, inc=1, device_id=place, device_id_type=MESH))
    for copy in loads + constants:
        copy.start()
    for c in range(6):
        stress[c] = jnp.zeros((8, NZ), jnp.float32)

    for copy in loads:
        copy.wait()

    east, west = wrap(gx + 1, nx), wrap(gx + nx - 1, nx)
    north, south = wrap(gy + 1, ny), wrap(gy + ny - 1, ny)
    side_x = {1: east, -1: west}
    side_y = {1: north, -1: south}
    slot = {1: 0, -1: 1}

    def remote(src, dst, step, number, place):
        return pltpu.make_async_remote_copy(
            src_ref=src,
            dst_ref=dst,
            send_sem=halo_send.at[step, number],
            recv_sem=halo_recv.at[step, number],
            device_id=place,
            device_id_type=MESH,
        )

    def wide():
        number = iter(range(WIDE))

        def to(ref, src, dst, spot):
            return pltpu.make_async_remote_copy(
                src_ref=ref.at[src],
                dst_ref=ref.at[dst] if ref is not row_out else row_in.at[dst],
                send_sem=wide_send.at[at := next(number)],
                recv_sem=wide_recv.at[at],
                device_id=spot,
                device_id_type=MESH,
            )

        every = slice(None)
        across, along = [], []
        for sign in (1, -1):
            spot = (side_x[sign], gy)
            if sign == 1:
                parts = [(pl.ds(0, UP), width + PAD, PAD), (pl.ds(0, STAY), width + 1, 1), (pl.ds(0, 19), width, 0)]
                rows = [(pl.ds(0, 1), width, 0, 3), (pl.ds(1, 3), width, 0, 2), (pl.ds(4, 1), width, 0, 1)]
                fields = (pl.ds(width, PAD), pl.ds(0, PAD))
            else:
                top = width + PAD
                parts = [
                    (pl.ds(STAY, UP), 1, top - 1), (pl.ds(UP, STAY), PAD, top), (pl.ds(0, 19), PAD + 1, top + 1)
                ]
                rows = [
                    (pl.ds(4, 1), 1, top - 1, 3), (pl.ds(1, 3), PAD, top, 2), (pl.ds(0, 1), PAD + 1, top + 1, 1)
                ]
                fields = (pl.ds(PAD, PAD), pl.ds(top, PAD))
            for which, here, there in parts:
                across.append(to(state, (1, which, pl.ds(here, 1)), (1, which, pl.ds(there, 1)), spot))
            for which, here, there, size in rows:
                src, dst = pl.ds(here, size), pl.ds(there, size)
                if ny == 2:
                    across.append(to(row_out, (1, every, which, src), (1, every, which, dst), (side_x[sign], north)))
                else:
                    for turn in (1, -1):
                        t = slot[turn]
                        diagonal = (side_x[sign], side_y[turn])
                        across.append(to(row_out, (1, t, which, src), (1, t, which, dst), diagonal))
            across.append(to(label, (fields[0],), (fields[1],), spot))
            across.append(to(drive, (every, fields[0]), (every, fields[1]), spot))
        for which, first in ((pl.ds(0, 1), PAD + 1), (pl.ds(1, 3), PAD), (pl.ds(4, 1), PAD - 1)):
            part = pl.ds(first, width)
            if ny == 2:
                along.append(to(row_out, (1, every, which, part), (1, every, which, part), (gx, north)))
            else:
                for turn in (1, -1):
                    t = slot[turn]
                    along.append(to(row_out, (1, t, which, part), (1, t, which, part), (gx, side_y[turn])))
        return across, along

    def lines_along(step):
        if ny == 2:
            return [remote(row_out.at[step + 1], row_in.at[step + 1], step, 2, (gx, north))]
        return [
            remote(row_out.at[step + 1, slot[sign]], row_in.at[step + 1, slot[sign]], step, 2 + slot[sign],
                   (gx, side_y[sign]))
            for sign in (1, -1)
        ]

    def halo(step):
        faces = []
        for sign in (1, -1):
            s = slot[sign]
            faces.append(remote(face_out.at[s], face_in.at[s], step, s, (side_x[sign], gy)))
            if ny == 2:
                faces.append(remote(edge_out.at[s], edge_in.at[s], step, 4 + s, (side_x[sign], north)))
                continue
            for turn in (1, -1):
                t = slot[turn]
                faces.append(
                    remote(edge_out.at[s, t], edge_in.at[s, t], step, 4 + 2 * s + t, (side_x[sign], side_y[turn]))
                )
        return faces

    row_id = lax.broadcasted_iota(jnp.int32, (8, NZ), 0)

    def read(step, i, p):
        cx, cy, _ = VELOCITY[i]
        if step == 0:
            return raw[i, p]
        outside = step == STEPS and ((cx == 1 and p == 0) or (cx == -1 and p == width - 1))
        if outside:
            value = face_in[slot[cx], CROSS[0, cx].index(i)]
        else:
            value = state[step, KEPT[i], p + PAD]
        if cy:
            if outside:
                row = edge_in[slot[cx], slot[cy]]
            else:
                row = row_in[step, slot[cy], CROSS[1, cy].index(i), p + PAD]
            value = jnp.where(row_id == (0 if cy == 1 else 7), jnp.broadcast_to(row, (8, NZ)), value)
        return value

    def write(step, i, p, value):
        cx, cy, cz = VELOCITY[i]
        to = p + cx
        last = step == STEPS - 1
        beyond = {0: 1, 1: 1, 2: 0, 3: 0}[step]
        outside = to < -beyond or to >= width + beyond
        if outside and not last:
            return
        if cz:
            value = pltpu.roll(value, cz % NZ, 1)
        if cy:
            value = pltpu.roll(value, cy % 8, 0)
            line = value[0:1] if cy == 1 else value[7:8]
        if outside:
            face_out[slot[cx], CROSS[0, cx].index(i)] = value
            if cy:
                edge_out[slot[cx], slot[cy]] = line
        else:
            state[step + 1, KEPT[i], to + PAD] = value
            if cy:
                row_out[step + 1, slot[cy], CROSS[1, cy].index(i), to + PAD] = line

    def send_copy(far, place):
        return pltpu.make_async_remote_copy(
            src_ref=message.at[far],
            dst_ref=arrived.at[far],
            send_sem=slow_send,
            recv_sem=slow_recv,
            device_id=place,
            device_id_type=MESH,
        )

    def phase_of(step):
        quarter = math.cos(math.pi / 4.0)
        return jnp.where((step == 0) | (step == STEPS - 1), quarter, -quarter)

    def measure(step, planes):
        total = [None] * 6
        held = []
        for p in planes:
            f = [read(step, i, p) for i in range(19)]
            rho, j = moments(f)
            inverse = 1.0 / rho
            held.append((p, f, rho, j, inverse))
            if p < 0 or p >= width:
                continue
            thin = jnp.where(label[p + PAD] == 2, 0.0, inverse)
            scaled = [one * thin for one in j]
            for c, (a, b) in enumerate(PAIRS):
                term = scaled[a] * j[b]
                total[c] = term if total[c] is None else total[c] + term
        for c in range(6):
            if total[c] is not None:
                stress[c] += total[c]
        return held

    def finish(step, held):
        phase = phase_of(step)
        for p, f, rho, j, inverse in held:
            second = label[p + PAD] == 1
            omega = jnp.where(second, 1.1, 1.6)
            strength = jnp.where(second, 0.6 * phase, phase)
            push = [strength * drive[a, p + PAD] for a in range(3)]
            post = collide(f, rho, j, inverse, 1.0 - omega, omega, push, label[p + PAD] == 2)
            for i in range(19):
                write(step, i, p, post[i])

    def advance(step, planes):
        for p in planes:
            finish(step, measure(step, [p]))

    advance(0, range(width))
    pl.semaphore_wait(barrier, count - 1)
    across, along = wide()
    for copy in across + along:
        copy.start()
    for copy in along:
        copy.wait_recv()
    advance(1, range(1, width - 1))
    for copy in across:
        copy.wait_recv()
    advance(1, [0, width - 1, -1, width, -2, width + 1])
    rows = lines_along(1)
    for copy in rows:
        copy.start()
    for copy in rows:
        copy.wait_recv()
    advance(2, range(-1, width + 1))
    rows = lines_along(2)
    for copy in rows:
        copy.start()
    for copy in constants:
        copy.wait()
    for copy in rows:
        copy.wait_recv()
    step = STEPS - 1
    held = measure(step, range(width))
    plain = dot(stress[:EVEN].reshape(8 * EVEN, NZ), forward[0])
    turned = dot(stress[EVEN:].reshape(8 * (6 - EVEN), NZ), forward[1])
    finish(step, held)
    last = halo(step) + lines_along(step)
    for copy in last:
        copy.start()

    lines = []
    for c in range(6):
        tile = plain[8 * c : 8 * c + 8] if c < EVEN else turned[8 * (c - EVEN) : 8 * (c - EVEN) + 8]
        tile = tile + pltpu.roll(tile, 7, 0)
        tile = tile + pltpu.roll(tile, 6, 0)
        lines.append(jnp.broadcast_to(tile[0:1], (8, NZ)))
        lines.append(jnp.broadcast_to(tile[4:5], (8, NZ)))

    def group(g):
        value = lines[0] * table[g, 0]
        for k in range(1, 12):
            value = value + lines[k] * table[g, k]
        for k in range(4):
            message[4 * g + k] = value[2 * k : 2 * k + 2]

    if count <= 64:
        for g in range(count // 4):
            group(g)
    else:
        def each(g, carry):
            group(g)
            return carry

        lax.fori_loop(0, count // 4, each, 0)
    over_others(lambda far, place: send_copy(far, place).start())

    for copy in last:
        copy.wait_recv()
    for p in range(width):
        f = [None] + [read(STEPS, i, p) for i in range(1, 19)]
        for axis in range(3):
            value = None
            for i in range(1, 19):
                c = VELOCITY[i][axis]
                if c:
                    value = c * f[i] if value is None else value + f[i] if c > 0 else value - f[i]
            momentum[axis, p] = value
    for copy in across + along + lines_along(1) + lines_along(2) + last:
        copy.wait_send()

    rest = pl.ds(1, count - 1)
    pltpu.make_async_copy(message.at[rest], arrived.at[rest], slow_recv).wait()
    spectrum = message[0]
    if count <= 64:
        for far in range(1, count):
            spectrum = spectrum + arrived[far]
    else:
        spectrum = lax.fori_loop(1, count, lambda far, value: value + arrived[far], spectrum)
    upper = jnp.broadcast_to(spectrum[0:1], (8, NZ))
    lower = jnp.broadcast_to(spectrum[1:2], (8, NZ))
    lane = lax.broadcasted_iota(jnp.int32, (8, NZ), 1)
    slow_z = NZ // CUT
    block = row_id % 2 + jnp.where(row_id >= 4, 2, 0)
    low = slow_z * block
    spread = jnp.where((row_id == 2) | (row_id == 3), lower, upper)
    spread = jnp.where((lane >= low) & (lane < low + slow_z), spread, 0.0)
    result = dot(spread, inverse_z[...])
    for a in range(3):
        running_ref[a, 0] = result[2 * a : 2 * a + 2, :slow_z]
    pltpu.make_async_copy(arrived.at[rest], message.at[rest], slow_send).wait()


def local(nx, ny, constants, pops, label, drive):
    width, height = pops.shape[1], pops.shape[2]
    count = nx * ny
    send, forward, inverse = constants
    anywhere = pl.BlockSpec(memory_space=pltpu.HBM)
    f32 = jnp.float32
    return pl.pallas_call(
        functools.partial(kernel, nx, ny),
        out_shape=(
            pltpu.VMEM((3, width, height, NZ), f32),
            pltpu.VMEM((3, width // CUT, height // CUT, NZ // CUT), f32),
        ),
        in_specs=[anywhere] * 6,
        out_specs=(pl.BlockSpec(memory_space=pltpu.VMEM),) * 2,
        scratch_shapes=[
            pltpu.VMEM((19, width, height, NZ), f32),
            pltpu.VMEM((STEPS + 1, 19, width + 2 * PAD, height, NZ), f32),
            pltpu.VMEM((6, height, NZ), f32),
            pltpu.VMEM((width + 2 * PAD, height, NZ), jnp.int32),
            pltpu.VMEM((3, width + 2 * PAD, height, NZ), f32),
            pltpu.VMEM(send.shape, f32),
            pltpu.VMEM(forward.shape, forward.dtype),
            pltpu.VMEM(inverse.shape, inverse.dtype),
            pltpu.VMEM((2, 5, height, NZ), f32),
            pltpu.VMEM((2, 5, height, NZ), f32),
            pltpu.VMEM((STEPS + 1, 2, 5, width + 2 * PAD, 1, NZ), f32),
            pltpu.VMEM((STEPS + 1, 2, 5, width + 2 * PAD, 1, NZ), f32),
            pltpu.VMEM((2, 2, 1, NZ), f32),
            pltpu.VMEM((2, 2, 1, NZ), f32),
            pltpu.VMEM((count, 2, NZ), f32),
            pltpu.VMEM((count, 2, NZ), f32),
            pltpu.SemaphoreType.DMA((3,)),
            pltpu.SemaphoreType.DMA((3,)),
            pltpu.SemaphoreType.DMA((WIDE,)),
            pltpu.SemaphoreType.DMA((WIDE,)),
            pltpu.SemaphoreType.DMA((STEPS, MESSAGES)),
            pltpu.SemaphoreType.DMA((STEPS, MESSAGES)),
            pltpu.SemaphoreType.DMA,
            pltpu.SemaphoreType.DMA,
        ],
        compiler_params=pltpu.CompilerParams(
            collective_id=0, has_side_effects=True, vmem_limit_bytes=60 * 1024 * 1024
        ),
        name="cycle",
    )(pops, label, drive, send, forward, inverse)


def solution(mesh):
    nx, ny = mesh.shape["gx"], mesh.shape["gy"]
    constants = tuple(jnp.asarray(table) for table in tables(nx, ny))
    in_specs = (P(None, "gx", "gy", None), P("gx", "gy", None), P(None, "gx", "gy", None))
    out_specs = (P(None, "gx", "gy", None), P(None, "gx", "gy", None))
    return jax.shard_map(
        functools.partial(local, nx, ny, constants),
        mesh=mesh, in_specs=in_specs, out_specs=out_specs, check_vma=False,
    )
```

```python
import functools
import math

import jax
import jax.numpy as jnp
import numpy as np
from jax import lax
from jax.experimental import pallas as pl
from jax.experimental.pallas import tpu as pltpu
from jax.sharding import PartitionSpec as P

MESH = pl.DeviceIdType.MESH
NZ = 128
STEPS = 4
CUT = 4
VELOCITY = [
    (0, 0, 0),
    (1, 0, 0),
    (-1, 0, 0),
    (0, 1, 0),
    (0, -1, 0),
    (0, 0, 1),
    (0, 0, -1),
    (1, 1, 0),
    (-1, -1, 0),
    (1, -1, 0),
    (-1, 1, 0),
    (1, 0, 1),
    (-1, 0, -1),
    (1, 0, -1),
    (-1, 0, 1),
    (0, 1, 1),
    (0, -1, -1),
    (0, 1, -1),
    (0, -1, 1),
]
WEIGHTS = [1.0 / 3.0] + [1.0 / 18.0] * 6 + [1.0 / 36.0] * 12
SLOW_VISCOSITY = 0.0004
PAIRS = [(0, 0), (1, 1), (2, 2), (0, 1), (0, 2), (1, 2)]
EVEN = 4
ORDER = [i for sign in (1, 0, -1) for i in range(19) if VELOCITY[i][0] == sign]
KEPT = {i: n for n, i in enumerate(ORDER)}
UP, STAY = 5, 14
CROSS = {(axis, sign): [i for i in ORDER if VELOCITY[i][axis] == sign] for axis in (0, 1) for sign in (1, -1)}
PAD = 2
MESSAGES = 8
WIDE = 32


def wave_table(length):
    index = np.arange(length)
    return 2.0 * np.pi * np.where(index >= (length + 1) // 2, index - length, index) / length


def response(nx, ny, nz):
    waves = np.meshgrid(wave_table(nx), wave_table(ny), wave_table(nz), indexing="ij")
    square = waves[0] ** 2 + waves[1] ** 2 + waves[2] ** 2
    safe = np.where(square > 0, square, 1.0)
    out = np.zeros((3, 6, nx, ny, nz // 2 + 1), np.complex128)
    for c, (p, q) in enumerate(PAIRS):
        force = [np.zeros_like(square) for _ in range(3)]
        force[p] = force[p] + waves[q]
        if p != q:
            force[q] = force[q] + waves[p]
        inner = sum(waves[a] * force[a] for a in range(3))
        for a in range(3):
            gain = np.where(square > 0, (force[a] - waves[a] * inner / safe) / (SLOW_VISCOSITY * safe), 0.0)
            mirror = np.roll(gain[::-1, ::-1, ::-1], (1, 1, 1), (0, 1, 2))
            odd = 0.5 * (gain - mirror)
            out[a, c] = np.fft.ifft2(-1j * odd, axes=(0, 1))[:, :, : nz // 2 + 1]
    return out


def split(table):
    table = table.astype(np.float32)
    high = table.astype(jnp.bfloat16)
    low = (table - high.astype(np.float32)).astype(jnp.bfloat16)
    return np.concatenate([high, low], axis=1)


def tables(nx, ny):
    slow = NZ // CUT
    half = slow // 2
    green = response(nx, 2 * ny, slow)
    count = nx * ny
    send = np.zeros((count, 12, 2, 4, slow))
    place = {(0, 0): (0, 0), (0, 1): (0, 1), (2, 0): (0, 2), (2, 1): (0, 3), (1, 0): (1, 0), (1, 1): (1, 1)}
    far_x = np.arange(count) // ny
    far_y = np.arange(count) % ny
    for c in range(6):
        for half_y in range(2):
            for (a, to_y), (row, block) in place.items():
                g = green[a, c][far_x, (2 * far_y + to_y - half_y) % (2 * ny)]
                inside = g[:, 1:half]
                if a < 2:
                    inside = inside.real if c < EVEN else inside.imag
                else:
                    inside = inside.imag if c < EVEN else -inside.real
                send[:, 2 * c + half_y, row, block, : half + 1] = g.real
                send[:, 2 * c + half_y, row, block, 1:half] = inside
                send[:, 2 * c + half_y, row, block, half + 1 :] = inside
    send = send.reshape(count // 4, 4, 12, 2, NZ).transpose(0, 2, 1, 3, 4).reshape(count // 4, 12, 8, NZ)
    place_z = np.arange(slow)
    angle = 2.0 * np.pi * place_z[:, None] * np.arange(half + 1)[None, :] / slow
    cosine, sine = np.cos(angle), np.sin(angle)
    plain = np.concatenate([cosine, -sine[:, 1:half]], axis=1)
    turned = np.concatenate([cosine[:, :1], sine[:, 1:half], cosine[:, half:], cosine[:, 1:half]], axis=1)
    scale = 1.0 / (STEPS * CUT**3)
    forward = np.stack([split(np.repeat(np.tile(one, (1, 4)), CUT, axis=0) * scale) for one in (plain, turned)])
    edge = [cosine[:, :1], cosine[:, half:]]
    back = np.concatenate([edge[0], 2 * cosine[:, 1:half], edge[1], -2 * sine[:, 1:half]], axis=1).T / slow
    back_turned = np.concatenate([edge[0], -2 * sine[:, 1:half], edge[1], -2 * cosine[:, 1:half]], axis=1).T / slow
    inverse = np.concatenate([back, back, back_turned, back_turned], axis=0)
    inverse = split(np.concatenate([inverse, np.zeros((NZ, NZ - slow))], axis=1))
    return send.astype(np.float32), forward, inverse


def dot(left, right):
    rows = left.shape[0]
    high = left.astype(jnp.bfloat16).astype(jnp.float32)
    parts = jnp.concatenate([high, left - high], axis=0).astype(jnp.bfloat16)
    both = jnp.dot(parts, right, preferred_element_type=jnp.float32)
    return both[:rows, :NZ] + (both[:rows, NZ:] + both[rows:, :NZ])


def moments(f):
    rho = f[0]
    for i in range(1, 19):
        rho = rho + f[i]
    j = []
    for axis in range(3):
        plus = [f[i] for i in range(19) if VELOCITY[i][axis] == 1]
        minus = [f[i] for i in range(19) if VELOCITY[i][axis] == -1]
        total = plus[0] - minus[0]
        for one, other in zip(plus[1:], minus[1:]):
            total = total + (one - other)
        j.append(total)
    return rho, j


def collide(f, rho, j, inverse, keep, omega, push, solid):
    speed = [one * inverse for one in j]
    square = speed[0] * speed[0] + speed[1] * speed[1] + speed[2] * speed[2]
    weight = omega * rho
    base = weight * (1.0 - 1.5 * square)
    quad = 4.5 * weight
    lead = [3.0 * (omega * j[a] + push[a]) for a in range(3)]
    post = [None] * 19
    post[0] = jnp.where(solid, f[0], keep * f[0] + WEIGHTS[0] * base)
    for i in range(1, 19, 2):
        along = linear = None
        for axis in range(3):
            c = VELOCITY[i][axis]
            if c:
                along = c * speed[axis] if along is None else along + speed[axis] if c > 0 else along - speed[axis]
                linear = c * lead[axis] if linear is None else linear + lead[axis] if c > 0 else linear - lead[axis]
        even = WEIGHTS[i] * (base + quad * (along * along))
        odd = WEIGHTS[i] * linear
        post[i] = jnp.where(solid, f[i + 1], keep * f[i] + (even + odd))
        post[i + 1] = jnp.where(solid, f[i], keep * f[i + 1] + (even - odd))
    return post


def kernel(
    nx, ny, pops_hbm, label_hbm, drive_hbm, table_hbm, forward_hbm, inverse_hbm, momentum, running_ref,
    raw, state, stress, label, drive, table, forward, inverse_z, face_out, face_in, row_out, row_in, edge_out, edge_in,
    message, arrived, load_sem, const_sem, wide_send, wide_recv, halo_send, halo_recv, slow_send, slow_recv,
):
    width = raw.shape[1]
    own = pl.ds(PAD, width)
    gx = lax.axis_index("gx")
    gy = lax.axis_index("gy")
    count = nx * ny

    loads = [
        pltpu.make_async_copy(pops_hbm, raw, load_sem.at[0]),
        pltpu.make_async_copy(label_hbm, label.at[own], load_sem.at[1]),
        pltpu.make_async_copy(drive_hbm, drive.at[:, own], load_sem.at[2]),
    ]
    constants = [
        pltpu.make_async_copy(table_hbm, table, const_sem.at[0]),
        pltpu.make_async_copy(forward_hbm, forward, const_sem.at[1]),
        pltpu.make_async_copy(inverse_hbm, inverse_z, const_sem.at[2]),
    ]
    def wrap(at, size):
        return jnp.where(at >= size, at - size, at)

    def over_others(body):
        for dy in range(1, ny):
            body(dy, (gx, wrap(gy + dy, ny)))

        def step(dx, carry):
            x = wrap(gx + dx, nx)
            for dy in range(ny):
                body(dx * ny + dy, (x, wrap(gy + dy, ny)))
            return carry

        lax.fori_loop(1, nx, step, 0)

    barrier = pltpu.get_barrier_semaphore()
    over_others(lambda far, place: pl.semaphore_signal(barrier, inc=1, device_id=place, device_id_type=MESH))
    for copy in loads + constants:
        copy.start()
    for c in range(6):
        stress[c] = jnp.zeros((8, NZ), jnp.float32)

    for copy in loads:
        copy.wait()

    east, west = wrap(gx + 1, nx), wrap(gx + nx - 1, nx)
    north, south = wrap(gy + 1, ny), wrap(gy + ny - 1, ny)
    side_x = {1: east, -1: west}
    side_y = {1: north, -1: south}
    slot = {1: 0, -1: 1}

    def remote(src, dst, step, number, place):
        return pltpu.make_async_remote_copy(
            src_ref=src,
            dst_ref=dst,
            send_sem=halo_send.at[step, number],
            recv_sem=halo_recv.at[step, number],
            device_id=place,
            device_id_type=MESH,
        )

    def wide():
        number = iter(range(WIDE))

        def to(ref, src, dst, spot):
            return pltpu.make_async_remote_copy(
                src_ref=ref.at[src],
                dst_ref=ref.at[dst] if ref is not row_out else row_in.at[dst],
                send_sem=wide_send.at[at := next(number)],
                recv_sem=wide_recv.at[at],
                device_id=spot,
                device_id_type=MESH,
            )

        every = slice(None)
        stages, along = ([], [], []), []
        for sign in (1, -1):
            spot = (side_x[sign], gy)
            if sign == 1:
                parts = [(pl.ds(0, UP), width + PAD, PAD), (pl.ds(0, STAY), width + 1, 1), (pl.ds(0, 19), width, 0)]
                rows = [(pl.ds(0, 1), width, 0, 3), (pl.ds(1, 3), width, 0, 2), (pl.ds(4, 1), width, 0, 1)]
                fields = (pl.ds(width, PAD), pl.ds(0, PAD))
            else:
                top = width + PAD
                parts = [
                    (pl.ds(STAY, UP), 1, top - 1), (pl.ds(UP, STAY), PAD, top), (pl.ds(0, 19), PAD + 1, top + 1)
                ]
                rows = [
                    (pl.ds(4, 1), 1, top - 1, 3), (pl.ds(1, 3), PAD, top, 2), (pl.ds(0, 1), PAD + 1, top + 1, 1)
                ]
                fields = (pl.ds(PAD, PAD), pl.ds(top, PAD))
            for stage, (which, here, there) in zip(stages, parts):
                stage.append(to(state, (1, which, pl.ds(here, 1)), (1, which, pl.ds(there, 1)), spot))
            for stage, (which, here, there, size) in zip(stages, rows):
                src, dst = pl.ds(here, size), pl.ds(there, size)
                if ny == 2:
                    stage.append(to(row_out, (1, every, which, src), (1, every, which, dst), (side_x[sign], north)))
                else:
                    for turn in (1, -1):
                        t = slot[turn]
                        diagonal = (side_x[sign], side_y[turn])
                        stage.append(to(row_out, (1, t, which, src), (1, t, which, dst), diagonal))
            stages[1].append(to(label, (fields[0],), (fields[1],), spot))
            stages[1].append(to(drive, (every, fields[0]), (every, fields[1]), spot))
        for which, first in ((pl.ds(0, 1), PAD + 1), (pl.ds(1, 3), PAD), (pl.ds(4, 1), PAD - 1)):
            part = pl.ds(first, width)
            if ny == 2:
                along.append(to(row_out, (1, every, which, part), (1, every, which, part), (gx, north)))
            else:
                for turn in (1, -1):
                    t = slot[turn]
                    along.append(to(row_out, (1, t, which, part), (1, t, which, part), (gx, side_y[turn])))
        return stages, along

    def lines_along(step):
        beyond = 1 if step == 1 else 0
        part = pl.ds(PAD - beyond, width + 2 * beyond)
        every = slice(None)
        if ny == 2:
            where = (step + 1, every, every, part)
            return [remote(row_out.at[where], row_in.at[where], step, 2, (gx, north))]
        copies = []
        for sign in (1, -1):
            where = (step + 1, slot[sign], every, part)
            copies.append(remote(row_out.at[where], row_in.at[where], step, 2 + slot[sign], (gx, side_y[sign])))
        return copies

    def halo(step):
        faces = []
        for sign in (1, -1):
            s = slot[sign]
            faces.append(remote(face_out.at[s], face_in.at[s], step, s, (side_x[sign], gy)))
            if ny == 2:
                faces.append(remote(edge_out.at[s], edge_in.at[s], step, 4 + s, (side_x[sign], north)))
                continue
            for turn in (1, -1):
                t = slot[turn]
                faces.append(
                    remote(edge_out.at[s, t], edge_in.at[s, t], step, 4 + 2 * s + t, (side_x[sign], side_y[turn]))
                )
        return faces

    row_id = lax.broadcasted_iota(jnp.int32, (8, NZ), 0)

    def read(step, i, p):
        cx, cy, _ = VELOCITY[i]
        if step == 0:
            return raw[i, p]
        outside = step == STEPS and ((cx == 1 and p == 0) or (cx == -1 and p == width - 1))
        if outside:
            value = face_in[slot[cx], CROSS[0, cx].index(i)]
        else:
            value = state[step, KEPT[i], p + PAD]
        if cy:
            if outside:
                row = edge_in[slot[cx], slot[cy]]
            else:
                row = row_in[step, slot[cy], CROSS[1, cy].index(i), p + PAD]
            value = jnp.where(row_id == (0 if cy == 1 else 7), jnp.broadcast_to(row, (8, NZ)), value)
        return value

    def write(step, i, p, value):
        cx, cy, cz = VELOCITY[i]
        to = p + cx
        last = step == STEPS - 1
        beyond = {0: 1, 1: 1, 2: 0, 3: 0}[step]
        outside = to < -beyond or to >= width + beyond
        if outside and not last:
            return
        if cz:
            value = pltpu.roll(value, cz % NZ, 1)
        if cy:
            value = pltpu.roll(value, cy % 8, 0)
            line = value[0:1] if cy == 1 else value[7:8]
        if outside:
            face_out[slot[cx], CROSS[0, cx].index(i)] = value
            if cy:
                edge_out[slot[cx], slot[cy]] = line
        else:
            state[step + 1, KEPT[i], to + PAD] = value
            if cy:
                row_out[step + 1, slot[cy], CROSS[1, cy].index(i), to + PAD] = line

    def send_copy(far, place):
        return pltpu.make_async_remote_copy(
            src_ref=message.at[far],
            dst_ref=arrived.at[far],
            send_sem=slow_send,
            recv_sem=slow_recv,
            device_id=place,
            device_id_type=MESH,
        )

    def phase_of(step):
        quarter = math.cos(math.pi / 4.0)
        return jnp.where((step == 0) | (step == STEPS - 1), quarter, -quarter)

    def measure(step, planes):
        total = [None] * 6
        held = []
        for p in planes:
            f = [read(step, i, p) for i in range(19)]
            rho, j = moments(f)
            inverse = 1.0 / rho
            held.append((p, f, rho, j, inverse))
            if p < 0 or p >= width:
                continue
            thin = jnp.where(label[p + PAD] == 2, 0.0, inverse)
            scaled = [one * thin for one in j]
            for c, (a, b) in enumerate(PAIRS):
                term = scaled[a] * j[b]
                total[c] = term if total[c] is None else total[c] + term
        for c in range(6):
            if total[c] is not None:
                stress[c] += total[c]
        return held

    def finish(step, held):
        phase = phase_of(step)
        for p, f, rho, j, inverse in held:
            second = label[p + PAD] == 1
            omega = jnp.where(second, 1.1, 1.6)
            strength = jnp.where(second, 0.6 * phase, phase)
            push = [strength * drive[a, p + PAD] for a in range(3)]
            post = collide(f, rho, j, inverse, 1.0 - omega, omega, push, label[p + PAD] == 2)
            for i in range(19):
                write(step, i, p, post[i])

    def advance(step, planes):
        for p in planes:
            finish(step, measure(step, [p]))

    advance(0, range(width))
    pl.semaphore_wait(barrier, count - 1)
    stages, along = wide()
    for copy in stages[0] + along + stages[1] + stages[2]:
        copy.start()
    for copy in along:
        copy.wait_recv()
    advance(1, range(1, width - 1))
    for distance, stage in enumerate(stages):
        for copy in stage:
            copy.wait_recv()
        advance(1, [-distance, width - 1 + distance])
    rows = lines_along(1)
    for copy in rows:
        copy.start()
    for copy in rows:
        copy.wait_recv()
    advance(2, range(-1, width + 1))
    rows = lines_along(2)
    for copy in rows:
        copy.start()
    for copy in constants:
        copy.wait()
    for copy in rows:
        copy.wait_recv()
    step = STEPS - 1
    held = measure(step, range(width))
    plain = dot(stress[:EVEN].reshape(8 * EVEN, NZ), forward[0])
    turned = dot(stress[EVEN:].reshape(8 * (6 - EVEN), NZ), forward[1])
    finish(step, held)
    last = halo(step) + lines_along(step)
    for copy in last:
        copy.start()

    lines = []
    for c in range(6):
        tile = plain[8 * c : 8 * c + 8] if c < EVEN else turned[8 * (c - EVEN) : 8 * (c - EVEN) + 8]
        tile = tile + pltpu.roll(tile, 7, 0)
        tile = tile + pltpu.roll(tile, 6, 0)
        lines.append(jnp.broadcast_to(tile[0:1], (8, NZ)))
        lines.append(jnp.broadcast_to(tile[4:5], (8, NZ)))

    def group(g):
        value = lines[0] * table[g, 0]
        for k in range(1, 12):
            value = value + lines[k] * table[g, k]
        for k in range(4):
            message[4 * g + k] = value[2 * k : 2 * k + 2]

    if count <= 64:
        for g in range(count // 4):
            group(g)
    else:
        def each(g, carry):
            group(g)
            return carry

        lax.fori_loop(0, count // 4, each, 0)
    over_others(lambda far, place: send_copy(far, place).start())

    for copy in last:
        copy.wait_recv()
    for p in range(width):
        f = [None] + [read(STEPS, i, p) for i in range(1, 19)]
        for axis in range(3):
            value = None
            for i in range(1, 19):
                c = VELOCITY[i][axis]
                if c:
                    value = c * f[i] if value is None else value + f[i] if c > 0 else value - f[i]
            momentum[axis, p] = value
    for copy in stages[0] + stages[1] + stages[2] + along + lines_along(1) + lines_along(2) + last:
        copy.wait_send()

    rest = pl.ds(1, count - 1)
    pltpu.make_async_copy(message.at[rest], arrived.at[rest], slow_recv).wait()
    spectrum = message[0]
    if count <= 64:
        for far in range(1, count):
            spectrum = spectrum + arrived[far]
    else:
        spectrum = lax.fori_loop(1, count, lambda far, value: value + arrived[far], spectrum)
    upper = jnp.broadcast_to(spectrum[0:1], (8, NZ))
    lower = jnp.broadcast_to(spectrum[1:2], (8, NZ))
    lane = lax.broadcasted_iota(jnp.int32, (8, NZ), 1)
    slow_z = NZ // CUT
    block = row_id % 2 + jnp.where(row_id >= 4, 2, 0)
    low = slow_z * block
    spread = jnp.where((row_id == 2) | (row_id == 3), lower, upper)
    spread = jnp.where((lane >= low) & (lane < low + slow_z), spread, 0.0)
    result = dot(spread, inverse_z[...])
    for a in range(3):
        running_ref[a, 0] = result[2 * a : 2 * a + 2, :slow_z]
    pltpu.make_async_copy(arrived.at[rest], message.at[rest], slow_send).wait()


def local(nx, ny, constants, pops, label, drive):
    width, height = pops.shape[1], pops.shape[2]
    count = nx * ny
    send, forward, inverse = constants
    anywhere = pl.BlockSpec(memory_space=pltpu.HBM)
    f32 = jnp.float32
    return pl.pallas_call(
        functools.partial(kernel, nx, ny),
        out_shape=(
            pltpu.VMEM((3, width, height, NZ), f32),
            pltpu.VMEM((3, width // CUT, height // CUT, NZ // CUT), f32),
        ),
        in_specs=[anywhere] * 6,
        out_specs=(pl.BlockSpec(memory_space=pltpu.VMEM),) * 2,
        scratch_shapes=[
            pltpu.VMEM((19, width, height, NZ), f32),
            pltpu.VMEM((STEPS + 1, 19, width + 2 * PAD, height, NZ), f32),
            pltpu.VMEM((6, height, NZ), f32),
            pltpu.VMEM((width + 2 * PAD, height, NZ), jnp.int32),
            pltpu.VMEM((3, width + 2 * PAD, height, NZ), f32),
            pltpu.VMEM(send.shape, f32),
            pltpu.VMEM(forward.shape, forward.dtype),
            pltpu.VMEM(inverse.shape, inverse.dtype),
            pltpu.VMEM((2, 5, height, NZ), f32),
            pltpu.VMEM((2, 5, height, NZ), f32),
            pltpu.VMEM((STEPS + 1, 2, 5, width + 2 * PAD, 1, NZ), f32),
            pltpu.VMEM((STEPS + 1, 2, 5, width + 2 * PAD, 1, NZ), f32),
            pltpu.VMEM((2, 2, 1, NZ), f32),
            pltpu.VMEM((2, 2, 1, NZ), f32),
            pltpu.VMEM((count, 2, NZ), f32),
            pltpu.VMEM((count, 2, NZ), f32),
            pltpu.SemaphoreType.DMA((3,)),
            pltpu.SemaphoreType.DMA((3,)),
            pltpu.SemaphoreType.DMA((WIDE,)),
            pltpu.SemaphoreType.DMA((WIDE,)),
            pltpu.SemaphoreType.DMA((STEPS, MESSAGES)),
            pltpu.SemaphoreType.DMA((STEPS, MESSAGES)),
            pltpu.SemaphoreType.DMA,
            pltpu.SemaphoreType.DMA,
        ],
        compiler_params=pltpu.CompilerParams(
            collective_id=0, has_side_effects=True, vmem_limit_bytes=60 * 1024 * 1024
        ),
        name="cycle",
    )(pops, label, drive, send, forward, inverse)


def solution(mesh):
    nx, ny = mesh.shape["gx"], mesh.shape["gy"]
    constants = tuple(jnp.asarray(table) for table in tables(nx, ny))
    in_specs = (P(None, "gx", "gy", None), P("gx", "gy", None), P(None, "gx", "gy", None))
    out_specs = (P(None, "gx", "gy", None), P(None, "gx", "gy", None))
    return jax.shard_map(
        functools.partial(local, nx, ny, constants),
        mesh=mesh, in_specs=in_specs, out_specs=out_specs, check_vma=False,
    )
```

```python
import functools
import math

import jax
import jax.numpy as jnp
import numpy as np
from jax import lax
from jax.experimental import pallas as pl
from jax.experimental.pallas import tpu as pltpu
from jax.sharding import PartitionSpec as P

MESH = pl.DeviceIdType.MESH
NZ = 128
STEPS = 4
CUT = 4
VELOCITY = [
    (0, 0, 0),
    (1, 0, 0),
    (-1, 0, 0),
    (0, 1, 0),
    (0, -1, 0),
    (0, 0, 1),
    (0, 0, -1),
    (1, 1, 0),
    (-1, -1, 0),
    (1, -1, 0),
    (-1, 1, 0),
    (1, 0, 1),
    (-1, 0, -1),
    (1, 0, -1),
    (-1, 0, 1),
    (0, 1, 1),
    (0, -1, -1),
    (0, 1, -1),
    (0, -1, 1),
]
WEIGHTS = [1.0 / 3.0] + [1.0 / 18.0] * 6 + [1.0 / 36.0] * 12
SLOW_VISCOSITY = 0.0004
PAIRS = [(0, 0), (1, 1), (2, 2), (0, 1), (0, 2), (1, 2)]
EVEN = 4
ORDER = [i for sign in (1, 0, -1) for i in range(19) if VELOCITY[i][0] == sign]
KEPT = {i: n for n, i in enumerate(ORDER)}
UP, STAY = 5, 14
CROSS = {(axis, sign): [i for i in ORDER if VELOCITY[i][axis] == sign] for axis in (0, 1) for sign in (1, -1)}
PAD = 2
MESSAGES = 8
WIDE = 32


def wave_table(length):
    index = np.arange(length)
    return 2.0 * np.pi * np.where(index >= (length + 1) // 2, index - length, index) / length


def response(nx, ny, nz):
    waves = np.meshgrid(wave_table(nx), wave_table(ny), wave_table(nz), indexing="ij")
    square = waves[0] ** 2 + waves[1] ** 2 + waves[2] ** 2
    safe = np.where(square > 0, square, 1.0)
    out = np.zeros((3, 6, nx, ny, nz // 2 + 1), np.complex128)
    for c, (p, q) in enumerate(PAIRS):
        force = [np.zeros_like(square) for _ in range(3)]
        force[p] = force[p] + waves[q]
        if p != q:
            force[q] = force[q] + waves[p]
        inner = sum(waves[a] * force[a] for a in range(3))
        for a in range(3):
            gain = np.where(square > 0, (force[a] - waves[a] * inner / safe) / (SLOW_VISCOSITY * safe), 0.0)
            mirror = np.roll(gain[::-1, ::-1, ::-1], (1, 1, 1), (0, 1, 2))
            odd = 0.5 * (gain - mirror)
            out[a, c] = np.fft.ifft2(-1j * odd, axes=(0, 1))[:, :, : nz // 2 + 1]
    return out


def split(table):
    table = table.astype(np.float32)
    high = table.astype(jnp.bfloat16)
    low = (table - high.astype(np.float32)).astype(jnp.bfloat16)
    return np.concatenate([high, low], axis=1)


def tables(nx, ny):
    slow = NZ // CUT
    half = slow // 2
    green = response(nx, 2 * ny, slow)
    count = nx * ny
    send = np.zeros((count, 12, 2, 4, slow))
    place = {(0, 0): (0, 0), (0, 1): (0, 1), (2, 0): (0, 2), (2, 1): (0, 3), (1, 0): (1, 0), (1, 1): (1, 1)}
    far_x = np.arange(count) // ny
    far_y = np.arange(count) % ny
    for c in range(6):
        for half_y in range(2):
            for (a, to_y), (row, block) in place.items():
                g = green[a, c][far_x, (2 * far_y + to_y - half_y) % (2 * ny)]
                inside = g[:, 1:half]
                if a < 2:
                    inside = inside.real if c < EVEN else inside.imag
                else:
                    inside = inside.imag if c < EVEN else -inside.real
                send[:, 2 * c + half_y, row, block, : half + 1] = g.real
                send[:, 2 * c + half_y, row, block, 1:half] = inside
                send[:, 2 * c + half_y, row, block, half + 1 :] = inside
    send = send.reshape(count // 4, 4, 12, 2, NZ).transpose(0, 2, 1, 3, 4).reshape(count // 4, 12, 8, NZ)
    place_z = np.arange(slow)
    angle = 2.0 * np.pi * place_z[:, None] * np.arange(half + 1)[None, :] / slow
    cosine, sine = np.cos(angle), np.sin(angle)
    plain = np.concatenate([cosine, -sine[:, 1:half]], axis=1)
    turned = np.concatenate([cosine[:, :1], sine[:, 1:half], cosine[:, half:], cosine[:, 1:half]], axis=1)
    scale = 1.0 / (STEPS * CUT**3)
    forward = np.stack([split(np.repeat(np.tile(one, (1, 4)), CUT, axis=0) * scale) for one in (plain, turned)])
    edge = [cosine[:, :1], cosine[:, half:]]
    back = np.concatenate([edge[0], 2 * cosine[:, 1:half], edge[1], -2 * sine[:, 1:half]], axis=1).T / slow
    back_turned = np.concatenate([edge[0], -2 * sine[:, 1:half], edge[1], -2 * cosine[:, 1:half]], axis=1).T / slow
    inverse = np.concatenate([back, back, back_turned, back_turned], axis=0)
    inverse = split(np.concatenate([inverse, np.zeros((NZ, NZ - slow))], axis=1))
    return send.astype(np.float32), forward, inverse


def dot(left, right):
    rows = left.shape[0]
    high = left.astype(jnp.bfloat16).astype(jnp.float32)
    parts = jnp.concatenate([high, left - high], axis=0).astype(jnp.bfloat16)
    both = jnp.dot(parts, right, preferred_element_type=jnp.float32)
    return both[:rows, :NZ] + (both[:rows, NZ:] + both[rows:, :NZ])


def moments(f):
    rho = f[0]
    for i in range(1, 19):
        rho = rho + f[i]
    j = []
    for axis in range(3):
        plus = [f[i] for i in range(19) if VELOCITY[i][axis] == 1]
        minus = [f[i] for i in range(19) if VELOCITY[i][axis] == -1]
        total = plus[0] - minus[0]
        for one, other in zip(plus[1:], minus[1:]):
            total = total + (one - other)
        j.append(total)
    return rho, j


def collide(f, rho, j, inverse, keep, omega, push, solid):
    speed = [one * inverse for one in j]
    square = speed[0] * speed[0] + speed[1] * speed[1] + speed[2] * speed[2]
    weight = omega * rho
    base = weight * (1.0 - 1.5 * square)
    quad = 4.5 * weight
    lead = [3.0 * (omega * j[a] + push[a]) for a in range(3)]
    post = [None] * 19
    post[0] = jnp.where(solid, f[0], keep * f[0] + WEIGHTS[0] * base)
    for i in range(1, 19, 2):
        along = linear = None
        for axis in range(3):
            c = VELOCITY[i][axis]
            if c:
                along = c * speed[axis] if along is None else along + speed[axis] if c > 0 else along - speed[axis]
                linear = c * lead[axis] if linear is None else linear + lead[axis] if c > 0 else linear - lead[axis]
        even = WEIGHTS[i] * (base + quad * (along * along))
        odd = WEIGHTS[i] * linear
        post[i] = jnp.where(solid, f[i + 1], keep * f[i] + (even + odd))
        post[i + 1] = jnp.where(solid, f[i], keep * f[i + 1] + (even - odd))
    return post


def kernel(
    nx, ny, pops_hbm, label_hbm, drive_hbm, table_hbm, forward_hbm, inverse_hbm, momentum, running_ref,
    raw, state, stress, label, drive, table, forward, inverse_z, face_out, face_in, row_out, row_in, edge_out, edge_in,
    message, arrived, load_sem, const_sem, wide_send, wide_recv, halo_send, halo_recv, slow_send, slow_recv,
):
    width = raw.shape[1]
    own = pl.ds(PAD, width)
    gx = lax.axis_index("gx")
    gy = lax.axis_index("gy")
    count = nx * ny

    loads = [
        pltpu.make_async_copy(pops_hbm, raw, load_sem.at[0]),
        pltpu.make_async_copy(label_hbm, label.at[own], load_sem.at[1]),
        pltpu.make_async_copy(drive_hbm, drive.at[:, own], load_sem.at[2]),
    ]
    constants = [
        pltpu.make_async_copy(table_hbm, table, const_sem.at[0]),
        pltpu.make_async_copy(forward_hbm, forward, const_sem.at[1]),
        pltpu.make_async_copy(inverse_hbm, inverse_z, const_sem.at[2]),
    ]
    def wrap(at, size):
        return jnp.where(at >= size, at - size, at)

    def over_others(body):
        for dy in range(1, ny):
            body(dy, (gx, wrap(gy + dy, ny)))

        def step(dx, carry):
            x = wrap(gx + dx, nx)
            for dy in range(ny):
                body(dx * ny + dy, (x, wrap(gy + dy, ny)))
            return carry

        lax.fori_loop(1, nx, step, 0)

    barrier = pltpu.get_barrier_semaphore()
    over_others(lambda far, place: pl.semaphore_signal(barrier, inc=1, device_id=place, device_id_type=MESH))
    for copy in loads + constants:
        copy.start()
    for c in range(6):
        stress[c] = jnp.zeros((8, NZ), jnp.float32)

    for copy in loads:
        copy.wait()

    east, west = wrap(gx + 1, nx), wrap(gx + nx - 1, nx)
    north, south = wrap(gy + 1, ny), wrap(gy + ny - 1, ny)
    side_x = {1: east, -1: west}
    side_y = {1: north, -1: south}
    slot = {1: 0, -1: 1}

    def remote(src, dst, step, number, place):
        return pltpu.make_async_remote_copy(
            src_ref=src,
            dst_ref=dst,
            send_sem=halo_send.at[step, number],
            recv_sem=halo_recv.at[step, number],
            device_id=place,
            device_id_type=MESH,
        )

    def wide():
        number = iter(range(WIDE))

        def to(ref, src, dst, spot):
            return pltpu.make_async_remote_copy(
                src_ref=ref.at[src],
                dst_ref=ref.at[dst] if ref is not row_out else row_in.at[dst],
                send_sem=wide_send.at[at := next(number)],
                recv_sem=wide_recv.at[at],
                device_id=spot,
                device_id_type=MESH,
            )

        every = slice(None)
        stages, along = ([], [], []), []
        for sign in (1, -1):
            spot = (side_x[sign], gy)
            if sign == 1:
                parts = [(pl.ds(0, UP), width + PAD, PAD), (pl.ds(0, STAY), width + 1, 1), (pl.ds(0, 19), width, 0)]
                rows = [(pl.ds(0, 1), width, 0, 3), (pl.ds(1, 3), width, 0, 2), (pl.ds(4, 1), width, 0, 1)]
                fields = (pl.ds(width, PAD), pl.ds(0, PAD))
            else:
                top = width + PAD
                parts = [
                    (pl.ds(STAY, UP), 1, top - 1), (pl.ds(UP, STAY), PAD, top), (pl.ds(0, 19), PAD + 1, top + 1)
                ]
                rows = [
                    (pl.ds(4, 1), 1, top - 1, 3), (pl.ds(1, 3), PAD, top, 2), (pl.ds(0, 1), PAD + 1, top + 1, 1)
                ]
                fields = (pl.ds(PAD, PAD), pl.ds(top, PAD))
            for stage, (which, here, there) in zip(stages, parts):
                stage.append(to(state, (1, which, pl.ds(here, 1)), (1, which, pl.ds(there, 1)), spot))
            for stage, (which, here, there, size) in zip(stages, rows):
                src, dst = pl.ds(here, size), pl.ds(there, size)
                if ny == 2:
                    stage.append(to(row_out, (1, every, which, src), (1, every, which, dst), (side_x[sign], north)))
                else:
                    for turn in (1, -1):
                        t = slot[turn]
                        diagonal = (side_x[sign], side_y[turn])
                        stage.append(to(row_out, (1, t, which, src), (1, t, which, dst), diagonal))
            stages[1].append(to(label, (fields[0],), (fields[1],), spot))
            stages[1].append(to(drive, (every, fields[0]), (every, fields[1]), spot))
        for which, first in ((pl.ds(0, 1), PAD + 1), (pl.ds(1, 3), PAD), (pl.ds(4, 1), PAD - 1)):
            part = pl.ds(first, width)
            if ny == 2:
                along.append(to(row_out, (1, every, which, part), (1, every, which, part), (gx, north)))
            else:
                for turn in (1, -1):
                    t = slot[turn]
                    along.append(to(row_out, (1, t, which, part), (1, t, which, part), (gx, side_y[turn])))
        return stages, along

    def lines_along(step):
        beyond = 1 if step == 1 else 0
        part = pl.ds(PAD - beyond, width + 2 * beyond)
        every = slice(None)
        if ny == 2:
            where = (step + 1, every, every, part)
            return [remote(row_out.at[where], row_in.at[where], step, 2, (gx, north))]
        copies = []
        for sign in (1, -1):
            where = (step + 1, slot[sign], every, part)
            copies.append(remote(row_out.at[where], row_in.at[where], step, 2 + slot[sign], (gx, side_y[sign])))
        return copies

    def halo(step):
        faces = []
        for sign in (1, -1):
            s = slot[sign]
            faces.append(remote(face_out.at[s], face_in.at[s], step, s, (side_x[sign], gy)))
            if ny == 2:
                faces.append(remote(edge_out.at[s], edge_in.at[s], step, 4 + s, (side_x[sign], north)))
                continue
            for turn in (1, -1):
                t = slot[turn]
                faces.append(
                    remote(edge_out.at[s, t], edge_in.at[s, t], step, 4 + 2 * s + t, (side_x[sign], side_y[turn]))
                )
        return faces

    row_id = lax.broadcasted_iota(jnp.int32, (8, NZ), 0)

    def read(step, i, p):
        cx, cy, _ = VELOCITY[i]
        if step == 0:
            return raw[i, p]
        outside = step == STEPS and ((cx == 1 and p == 0) or (cx == -1 and p == width - 1))
        if outside:
            value = face_in[slot[cx], CROSS[0, cx].index(i)]
        else:
            value = state[step, KEPT[i], p + PAD]
        if cy:
            if outside:
                row = edge_in[slot[cx], slot[cy]]
            else:
                row = row_in[step, slot[cy], CROSS[1, cy].index(i), p + PAD]
            value = jnp.where(row_id == (0 if cy == 1 else 7), jnp.broadcast_to(row, (8, NZ)), value)
        return value

    def write(step, i, p, value):
        cx, cy, cz = VELOCITY[i]
        to = p + cx
        last = step == STEPS - 1
        beyond = {0: 1, 1: 1, 2: 0, 3: 0}[step]
        outside = to < -beyond or to >= width + beyond
        if outside and not last:
            return
        if cz:
            value = pltpu.roll(value, cz % NZ, 1)
        if cy:
            value = pltpu.roll(value, cy % 8, 0)
            line = value[0:1] if cy == 1 else value[7:8]
        if outside:
            face_out[slot[cx], CROSS[0, cx].index(i)] = value
            if cy:
                edge_out[slot[cx], slot[cy]] = line
        else:
            state[step + 1, KEPT[i], to + PAD] = value
            if cy:
                row_out[step + 1, slot[cy], CROSS[1, cy].index(i), to + PAD] = line

    def send_copy(far, place):
        return pltpu.make_async_remote_copy(
            src_ref=message.at[far],
            dst_ref=arrived.at[far],
            send_sem=slow_send,
            recv_sem=slow_recv,
            device_id=place,
            device_id_type=MESH,
        )

    def phase_of(step):
        quarter = math.cos(math.pi / 4.0)
        return jnp.where((step == 0) | (step == STEPS - 1), quarter, -quarter)

    def measure(step, planes):
        total = [None] * 6
        held = []
        for p in planes:
            f = [read(step, i, p) for i in range(19)]
            rho, j = moments(f)
            inverse = 1.0 / rho
            held.append((p, f, rho, j, inverse))
            if p < 0 or p >= width:
                continue
            thin = jnp.where(label[p + PAD] == 2, 0.0, inverse)
            scaled = [one * thin for one in j]
            for c, (a, b) in enumerate(PAIRS):
                term = scaled[a] * j[b]
                total[c] = term if total[c] is None else total[c] + term
        for c in range(6):
            if total[c] is not None:
                stress[c] += total[c]
        return held

    def finish(step, held):
        phase = phase_of(step)
        for p, f, rho, j, inverse in held:
            second = label[p + PAD] == 1
            omega = jnp.where(second, 1.1, 1.6)
            strength = jnp.where(second, 0.6 * phase, phase)
            push = [strength * drive[a, p + PAD] for a in range(3)]
            post = collide(f, rho, j, inverse, 1.0 - omega, omega, push, label[p + PAD] == 2)
            for i in range(19):
                write(step, i, p, post[i])

    def advance(step, planes):
        for p in planes:
            finish(step, measure(step, [p]))

    advance(0, range(width))
    pl.semaphore_wait(barrier, count - 1)
    stages, along = wide()
    for copy in stages[0] + along + stages[1] + stages[2]:
        copy.start()
    for copy in along:
        copy.wait_recv()
    advance(1, range(1, width - 1))
    for distance, stage in enumerate(stages):
        for copy in stage:
            copy.wait_recv()
        advance(1, [-distance, width - 1 + distance])
    rows = lines_along(1)
    for copy in rows:
        copy.start()
    for copy in rows:
        copy.wait_recv()
    advance(2, range(-1, width + 1))
    rows = lines_along(2)
    for copy in rows:
        copy.start()
    for copy in constants:
        copy.wait()
    for copy in rows:
        copy.wait_recv()
    step = STEPS - 1
    held = measure(step, range(width))
    plain = dot(stress[:EVEN].reshape(8 * EVEN, NZ), forward[0])
    turned = dot(stress[EVEN:].reshape(8 * (6 - EVEN), NZ), forward[1])
    finish(step, held)
    last = halo(step) + lines_along(step)
    lines = []
    for c in range(6):
        tile = plain[8 * c : 8 * c + 8] if c < EVEN else turned[8 * (c - EVEN) : 8 * (c - EVEN) + 8]
        tile = tile + pltpu.roll(tile, 7, 0)
        tile = tile + pltpu.roll(tile, 6, 0)
        lines.append(jnp.broadcast_to(tile[0:1], (8, NZ)))
        lines.append(jnp.broadcast_to(tile[4:5], (8, NZ)))

    def group(g):
        value = lines[0] * table[g, 0]
        for k in range(1, 12):
            value = value + lines[k] * table[g, k]
        for k in range(4):
            message[4 * g + k] = value[2 * k : 2 * k + 2]

    if count <= 64:
        for g in range(count // 4):
            group(g)
    else:
        def each(g, carry):
            group(g)
            return carry

        lax.fori_loop(0, count // 4, each, 0)
    over_others(lambda far, place: send_copy(far, place).start())
    for copy in last:
        copy.start()

    for copy in last:
        copy.wait_recv()
    for p in range(width):
        f = [None] + [read(STEPS, i, p) for i in range(1, 19)]
        for axis in range(3):
            value = None
            for i in range(1, 19):
                c = VELOCITY[i][axis]
                if c:
                    value = c * f[i] if value is None else value + f[i] if c > 0 else value - f[i]
            momentum[axis, p] = value
    for copy in stages[0] + stages[1] + stages[2] + along + lines_along(1) + lines_along(2) + last:
        copy.wait_send()

    rest = pl.ds(1, count - 1)
    pltpu.make_async_copy(message.at[rest], arrived.at[rest], slow_recv).wait()
    spectrum = message[0]
    if count <= 64:
        for far in range(1, count):
            spectrum = spectrum + arrived[far]
    else:
        spectrum = lax.fori_loop(1, count, lambda far, value: value + arrived[far], spectrum)
    upper = jnp.broadcast_to(spectrum[0:1], (8, NZ))
    lower = jnp.broadcast_to(spectrum[1:2], (8, NZ))
    lane = lax.broadcasted_iota(jnp.int32, (8, NZ), 1)
    slow_z = NZ // CUT
    block = row_id % 2 + jnp.where(row_id >= 4, 2, 0)
    low = slow_z * block
    spread = jnp.where((row_id == 2) | (row_id == 3), lower, upper)
    spread = jnp.where((lane >= low) & (lane < low + slow_z), spread, 0.0)
    result = dot(spread, inverse_z[...])
    for a in range(3):
        running_ref[a, 0] = result[2 * a : 2 * a + 2, :slow_z]
    pltpu.make_async_copy(arrived.at[rest], message.at[rest], slow_send).wait()


def local(nx, ny, constants, pops, label, drive):
    width, height = pops.shape[1], pops.shape[2]
    count = nx * ny
    send, forward, inverse = constants
    anywhere = pl.BlockSpec(memory_space=pltpu.HBM)
    f32 = jnp.float32
    return pl.pallas_call(
        functools.partial(kernel, nx, ny),
        out_shape=(
            pltpu.VMEM((3, width, height, NZ), f32),
            pltpu.VMEM((3, width // CUT, height // CUT, NZ // CUT), f32),
        ),
        in_specs=[anywhere] * 6,
        out_specs=(pl.BlockSpec(memory_space=pltpu.VMEM),) * 2,
        scratch_shapes=[
            pltpu.VMEM((19, width, height, NZ), f32),
            pltpu.VMEM((STEPS + 1, 19, width + 2 * PAD, height, NZ), f32),
            pltpu.VMEM((6, height, NZ), f32),
            pltpu.VMEM((width + 2 * PAD, height, NZ), jnp.int32),
            pltpu.VMEM((3, width + 2 * PAD, height, NZ), f32),
            pltpu.VMEM(send.shape, f32),
            pltpu.VMEM(forward.shape, forward.dtype),
            pltpu.VMEM(inverse.shape, inverse.dtype),
            pltpu.VMEM((2, 5, height, NZ), f32),
            pltpu.VMEM((2, 5, height, NZ), f32),
            pltpu.VMEM((STEPS + 1, 2, 5, width + 2 * PAD, 1, NZ), f32),
            pltpu.VMEM((STEPS + 1, 2, 5, width + 2 * PAD, 1, NZ), f32),
            pltpu.VMEM((2, 2, 1, NZ), f32),
            pltpu.VMEM((2, 2, 1, NZ), f32),
            pltpu.VMEM((count, 2, NZ), f32),
            pltpu.VMEM((count, 2, NZ), f32),
            pltpu.SemaphoreType.DMA((3,)),
            pltpu.SemaphoreType.DMA((3,)),
            pltpu.SemaphoreType.DMA((WIDE,)),
            pltpu.SemaphoreType.DMA((WIDE,)),
            pltpu.SemaphoreType.DMA((STEPS, MESSAGES)),
            pltpu.SemaphoreType.DMA((STEPS, MESSAGES)),
            pltpu.SemaphoreType.DMA,
            pltpu.SemaphoreType.DMA,
        ],
        compiler_params=pltpu.CompilerParams(
            collective_id=0, has_side_effects=True, vmem_limit_bytes=60 * 1024 * 1024
        ),
        name="cycle",
    )(pops, label, drive, send, forward, inverse)


def solution(mesh):
    nx, ny = mesh.shape["gx"], mesh.shape["gy"]
    constants = tuple(jnp.asarray(table) for table in tables(nx, ny))
    in_specs = (P(None, "gx", "gy", None), P("gx", "gy", None), P(None, "gx", "gy", None))
    out_specs = (P(None, "gx", "gy", None), P(None, "gx", "gy", None))
    return jax.shard_map(
        functools.partial(local, nx, ny, constants),
        mesh=mesh, in_specs=in_specs, out_specs=out_specs, check_vma=False,
    )
```
